512 devices in a mesh: ctx: 64 (over z, y), tp: 8 (over x, core).
Axes of the slice: x: 4, y: 4, z: 16, core: 2. Of those that a mesh axis runs over, the one named last changes fastest.
Arguments:
- query_in: bfloat16 [16384, 8192], P('ctx', 'tp'), may hold values from -6 to 6
- key_in: bfloat16 [16384, 8192], P('ctx', 'tp'), may hold values from -6 to 6
- value_in: bfloat16 [16384, 8192], P('ctx', 'tp'), may hold values from -6 to 6
- out_grad: bfloat16 [16384, 8192], P('ctx', 'tp'), may hold values from -400 to 400
- fill_counts: int32 [64], P('ctx'), may hold values from 192 to 256, as said below
- doc_starts: int32 [4], replicated, may hold values from 0 to 12287, as said below
- feat_taps: bfloat16 [3, 7, 8192], P(None, None, 'tp'), may hold values from -2 to 2
- mix_taps: bfloat16 [512, 128], P('tp'), may hold values from -0.5 to 0.5
- skip_gain: float32 [8192], P('tp'), may hold values from -4 to 4
Outputs:
- hyena_out: bfloat16 [16384, 8192], P('ctx', 'tp')
- query_grad: bfloat16 [16384, 8192], P('ctx', 'tp')
- key_grad: bfloat16 [16384, 8192], P('ctx', 'tp')
- value_grad: bfloat16 [16384, 8192], P('ctx', 'tp')
- mix_grad: float32 [512, 128], P('tp')
- skip_grad: float32 [8192], P('tp')
- feat_grad: float32 [3, 7, 8192], P(None, None, 'tp')
The draws below stay inside these ranges and needn't reach their ends.
Inputs may be any that keep to these rules, and one draw needn't show every extreme that they name: `fill_counts`: entry s is the number of filled slots of shard s; the filled slots are a shard's first ones. Some shard is full. `doc_starts`: strictly increasing; the first entry is 0.
All inputs are finite; a program needn't handle non-finite values.
Results may differ from the reference program's by a relative error of at most 0.0075.
Values may be sent and summed in bfloat16 or wider, within the bound.
A program may use at most 128 MiB of HBM per device.

```python
import math
import jax
import jax.numpy as jnp
from jax import lax

D = 8192
FILT = 128
SHORT = 7
ROWS = 256
DOCS = 4
SHARDS = 64
TOKENS = 16384
GROUPS = 512
N_TP = 8


def draw_fill_counts(key, part):
    subkeys = jax.random.split(jax.random.fold_in(key, 11), 2)
    counts = jax.random.randint(subkeys[0], (SHARDS,), 3 * ROWS // 4, ROWS + 1, dtype=jnp.int32)
    order = jax.random.permutation(subkeys[1], SHARDS)
    counts = counts.at[order[0]].set(ROWS)
    counts = counts.at[order[1]].set(3 * ROWS // 4)
    return counts.astype(jnp.int32)


def draw_doc_starts(key, part):
    limit = SHARDS * (3 * ROWS // 4)
    picked = jax.random.permutation(jax.random.fold_in(key, 23), limit - 2)[:DOCS - 2] + 1
    picked = jnp.sort(picked.astype(jnp.int32))
    return jnp.concatenate([jnp.zeros((1,), jnp.int32), picked, jnp.full((1,), limit - 1, jnp.int32)]).astype(jnp.int32)


def draw_out_grad(key, part):
    subkeys = jax.random.split(jax.random.fold_in(key, 37), 3)
    row_pos = jnp.arange(TOKENS, dtype=jnp.float32) / TOKENS
    col_pos = jnp.arange(D, dtype=jnp.float32) / D
    row_scale = (1.0 + 2.0 * row_pos) * jnp.exp(jax.random.uniform(subkeys[0], (TOKENS,), jnp.float32, -0.6, 0.6))
    col_scale = (1.0 + 2.0 * col_pos) * jnp.exp(jax.random.uniform(subkeys[1], (D,), jnp.float32, -0.6, 0.6))
    noise = jnp.clip(jax.random.normal(subkeys[2], (TOKENS, D), jnp.float32), -5.0, 5.0)
    return (noise * row_scale[:, None] * col_scale[None, :]).astype(jnp.bfloat16)


def levels(rng, extent, cuts, smallest, top_value):
    loudness, own = 1.0, jax.random.fold_in(rng, 6)
    for axis_at, shards_of in cuts:
        steps = jnp.exp(jax.random.uniform(jax.random.fold_in(own, axis_at), (shards_of,), jnp.float32, smallest / len(cuts), top_value / len(cuts)))
        loudness = loudness * jnp.repeat(steps, extent[axis_at] // shards_of).reshape([-1 if axis == axis_at else 1 for axis in range(len(extent))])
    return loudness


def bell_draw(rng, shape, scale, reach, cuts=(), kind=jnp.bfloat16):
    result = jax.random.normal(rng, shape, jnp.float32) * scale
    if len(cuts) > 0:
        result = levels(rng, shape, cuts, -0.22, 0.18) * result
    return jnp.clip(result, min=-reach, max=reach).astype(kind)


def setup_inputs(seed: int = 0) -> dict:
    streams_of = jax.random.split(jax.random.key(seed), 10)
    query_in = bell_draw(streams_of[0], (TOKENS, D), 1.0, 6.0, ((0, 64), (1, 8)))
    key_in = bell_draw(streams_of[1], (TOKENS, D), 1.0, 6.0, ((0, 64), (1, 8)))
    value_in = bell_draw(streams_of[2], (TOKENS, D), 1.0, 6.0, ((0, 64), (1, 8)))
    out_grad = draw_out_grad(jax.random.fold_in(streams_of[9], 71), 0)
    fill_counts = draw_fill_counts(jax.random.fold_in(streams_of[9], 71), 0)
    doc_starts = draw_doc_starts(jax.random.fold_in(streams_of[9], 71), 0)
    feat_taps = bell_draw(streams_of[6], (3, SHORT, D), SHORT ** -0.5, 2.0, ((2, 8),))
    mix_taps = bell_draw(streams_of[7], (GROUPS, FILT), FILT ** -0.5, 0.5, ((0, 8),))
    skip_gain = bell_draw(streams_of[8], (D,), 1.0, 4.0, ((0, 8),), jnp.float32)
    return {"query_in": query_in, "key_in": key_in, "value_in": value_in, "out_grad": out_grad, "fill_counts": fill_counts, "doc_starts": doc_starts, "feat_taps": feat_taps, "mix_taps": mix_taps, "skip_gain": skip_gain}


def doc_index(positions, doc_starts):
    counted = lax.optimization_barrier(jnp.sum((doc_starts[None, :] <= positions[:, None]).astype(jnp.int32), axis=1))
    return (counted - 1).astype(jnp.int32)

def banded(coeffs, block_rows):
    group_count, filter_len = coeffs.shape
    window = block_rows + filter_len - 1
    padded_row = jnp.concatenate([coeffs, jnp.zeros((group_count, window + 1 - filter_len), coeffs.dtype)], axis=1)
    tiled = jnp.broadcast_to(padded_row[:, None, :], (group_count, block_rows, window + 1))
    tiled = tiled.reshape(group_count, block_rows * (window + 1))
    return tiled[:, :block_rows * window].reshape(group_count, block_rows, window)

def diagonals(products, filter_len):
    group_count, block_rows, window = products.shape
    flat = jnp.concatenate([products.reshape(group_count, block_rows * window), jnp.zeros((group_count, block_rows), products.dtype)], axis=1)
    return lax.optimization_barrier(jnp.sum(flat.reshape(group_count, block_rows, window + 1)[:, :, :filter_len], axis=1))

def contract(form, left, right):
    return jnp.einsum(form, left.astype(jnp.float32), right.astype(jnp.float32))

def featurize(extended, doc_ext, weights):
    short_len = weights.shape[0]
    out_rows = extended.shape[0] - short_len + 1
    doc_out = doc_ext[short_len - 1:]
    accum = jnp.zeros((out_rows, extended.shape[1]), jnp.float32)
    for j in range(short_len):
        offset = short_len - 1 - j
        source = extended[offset:offset + out_rows].astype(jnp.float32)
        same_doc = (doc_out == doc_ext[offset:offset + out_rows])[:, None]
        accum = accum + jnp.where(same_doc, weights[j].astype(jnp.float32) * source, 0.0)
    return accum

def unfeaturize(extended, doc_ext, weights):
    short_len = weights.shape[0]
    out_rows = extended.shape[0] - short_len + 1
    doc_out = doc_ext[:out_rows]
    accum = jnp.zeros((out_rows, extended.shape[1]), jnp.float32)
    for j in range(short_len):
        source = extended[j:j + out_rows].astype(jnp.float32)
        same_doc = (doc_out == doc_ext[j:j + out_rows])[:, None]
        accum = accum + jnp.where(same_doc, weights[j].astype(jnp.float32) * source, 0.0)
    return accum

def feat_grads(extended, doc_ext, grads):
    out_rows = grads.shape[0]
    short_len = extended.shape[0] - out_rows + 1
    doc_out = doc_ext[short_len - 1:]
    pieces = []
    for j in range(short_len):
        offset = short_len - 1 - j
        source = extended[offset:offset + out_rows].astype(jnp.float32)
        same_doc = (doc_out == doc_ext[offset:offset + out_rows])[:, None]
        pieces.append(lax.optimization_barrier(jnp.sum(jnp.where(same_doc, source * grads.astype(jnp.float32), 0.0), axis=0)))
    return jnp.stack(pieces)

def mix_blocks(extended, doc_ext, band, leading):
    group_count, block_rows, window = band.shape
    filter_len = window - block_rows + 1
    channels = extended.shape[1]
    per_group = channels // group_count
    out_rows = extended.shape[0] - filter_len + 1

    def per_block(b):
        first = b * block_rows
        source = lax.dynamic_slice_in_dim(extended, first, window, 0).reshape(window, group_count, per_group)
        doc_src = lax.dynamic_slice_in_dim(doc_ext, first, window, 0)
        doc_out = doc_src[filter_len - 1:] if leading else doc_src[:block_rows]
        matrix = jnp.where((doc_out[:, None] == doc_src[None, :])[None], band, jnp.zeros((), band.dtype))
        return contract('gas,sgc->agc', matrix, source).reshape(block_rows, channels)
    blocks = lax.map(per_block, jnp.arange(out_rows // block_rows, dtype=jnp.int32))
    return blocks.reshape(out_rows, channels)

def grad_blocks(ext_grad, doc_back, ext_mix, doc_long, row_grads, band):
    group_count, block_rows, window = band.shape
    filter_len = window - block_rows + 1
    out_rows, channels = row_grads.shape
    per_group = channels // group_count

    def per_block(b):
        first = b * block_rows
        source = lax.dynamic_slice_in_dim(ext_grad, first, window, 0).reshape(window, group_count, per_group)
        doc_src = lax.dynamic_slice_in_dim(doc_back, first, window, 0)
        matrix = jnp.where((doc_src[:block_rows, None] == doc_src[None, :])[None], band, jnp.zeros((), band.dtype))
        back_rows = contract('gas,sgc->agc', matrix, source).reshape(block_rows, channels)
        mix_src = lax.dynamic_slice_in_dim(ext_mix, first, window, 0).reshape(window, group_count, per_group)
        doc_mix = lax.dynamic_slice_in_dim(doc_long, first, window, 0)
        own_rows = lax.dynamic_slice_in_dim(row_grads, first, block_rows, 0).reshape(block_rows, group_count, per_group)
        products = contract('agc,sgc->gas', own_rows, mix_src)
        products = jnp.where((doc_mix[filter_len - 1:, None] == doc_mix[None, :])[None], products, 0.0)
        return (back_rows, diagonals(products, filter_len))
    back_all, taps_all = lax.map(per_block, jnp.arange(out_rows // block_rows, dtype=jnp.int32))
    return (back_all.reshape(out_rows, channels), lax.optimization_barrier(jnp.sum(taps_all, axis=0))[:, ::-1])

def channel_block(query_in, key_in, value_in, out_grad, feat_taps, mix_taps, skip_gain, doc_ids):
    token_count, channels = query_in.shape
    short_len = feat_taps.shape[1]
    filter_len = mix_taps.shape[1]
    block_rows = math.gcd(ROWS, 128)
    doc_short = jnp.concatenate([jnp.full((short_len - 1,), -2, jnp.int32), doc_ids])
    pad_short = jnp.zeros((short_len - 1, channels), query_in.dtype)
    ext_q = jnp.concatenate([pad_short, query_in], axis=0)
    ext_k = jnp.concatenate([pad_short, key_in], axis=0)
    ext_v = jnp.concatenate([pad_short, value_in], axis=0)
    query = featurize(ext_q, doc_short, feat_taps[0])
    keys = featurize(ext_k, doc_short, feat_taps[1])
    values = featurize(ext_v, doc_short, feat_taps[2])
    mix_in = (keys * values).astype(jnp.bfloat16)
    doc_long = jnp.concatenate([jnp.full((filter_len - 1,), -2, jnp.int32), doc_ids])
    ext_mix = jnp.concatenate([jnp.zeros((filter_len - 1, channels), mix_in.dtype), mix_in], axis=0)
    mixed = mix_blocks(ext_mix, doc_long, banded(mix_taps[:, ::-1], block_rows), True)
    gated = mixed + skip_gain[None, :] * mix_in.astype(jnp.float32)
    hyena_out = (query * gated).astype(jnp.bfloat16)
    grad_f = out_grad.astype(jnp.float32)
    mix_grad_rows = (grad_f * query).astype(jnp.bfloat16)
    query_back = (grad_f * gated).astype(jnp.bfloat16)
    ext_grad = jnp.concatenate([mix_grad_rows, jnp.zeros((filter_len - 1, channels), mix_grad_rows.dtype)], axis=0)
    doc_back = jnp.concatenate([doc_ids, jnp.full((filter_len - 1,), -3, jnp.int32)])
    back_rows, taps_grad = grad_blocks(ext_grad, doc_back, ext_mix, doc_long, mix_grad_rows, banded(mix_taps, block_rows))
    mix_back = back_rows + skip_gain[None, :] * mix_grad_rows.astype(jnp.float32)
    key_back = (mix_back * values).astype(jnp.bfloat16)
    value_back = (mix_back * keys).astype(jnp.bfloat16)
    doc_near = doc_back[:token_count + short_len - 1]
    tail_pad = jnp.zeros((short_len - 1, channels), jnp.bfloat16)
    query_grad = unfeaturize(jnp.concatenate([query_back, tail_pad], axis=0), doc_near, feat_taps[0]).astype(jnp.bfloat16)
    key_grad = unfeaturize(jnp.concatenate([key_back, tail_pad], axis=0), doc_near, feat_taps[1]).astype(jnp.bfloat16)
    value_grad = unfeaturize(jnp.concatenate([value_back, tail_pad], axis=0), doc_near, feat_taps[2]).astype(jnp.bfloat16)
    feat = jnp.stack([feat_grads(ext_q, doc_short, query_back), feat_grads(ext_k, doc_short, key_back), feat_grads(ext_v, doc_short, value_back)])
    skip_part = lax.optimization_barrier(jnp.sum(mix_in.astype(jnp.float32) * mix_grad_rows.astype(jnp.float32), axis=0))
    return (hyena_out, query_grad, key_grad, value_grad, taps_grad, skip_part, feat)

def reference(query_in, key_in, value_in, out_grad, fill_counts, doc_starts, feat_taps, mix_taps, skip_gain):
    starts = (jnp.cumsum(fill_counts) - fill_counts).astype(jnp.int32)
    slot_pos = jnp.arange(ROWS, dtype=jnp.int32)
    is_valid = (slot_pos[None, :] < fill_counts[:, None]).reshape(TOKENS)
    slot_index = jnp.where(is_valid, (starts[:, None] + slot_pos[None, :]).reshape(TOKENS), TOKENS).astype(jnp.int32)
    gather_at = jnp.minimum(slot_index, TOKENS - 1).astype(jnp.int32)
    doc_ids = doc_index(jnp.arange(TOKENS, dtype=jnp.int32), doc_starts)
    channels = D // N_TP

    def to_blocks(source):
        stream = jnp.zeros_like(source).at[slot_index].set(source, mode='drop')
        return stream.reshape(TOKENS, N_TP, channels).transpose(1, 0, 2)

    def from_blocks(blocks):
        stream = blocks.transpose(1, 0, 2).reshape(TOKENS, D)
        return jnp.where(is_valid[:, None], stream[gather_at], jnp.zeros((), stream.dtype))
    feat_blocks = feat_taps.reshape(3, SHORT, N_TP, channels).transpose(2, 0, 1, 3)
    taps_blocks = mix_taps.reshape(N_TP, GROUPS // N_TP, FILT)
    skip_blocks = skip_gain.reshape(N_TP, channels)

    def run_block(operands):
        return channel_block(operands[0], operands[1], operands[2], operands[3], operands[4], operands[5], operands[6], doc_ids)
    results = lax.map(run_block, (to_blocks(query_in), to_blocks(key_in), to_blocks(value_in), to_blocks(out_grad), feat_blocks, taps_blocks, skip_blocks))
    hyena_out = from_blocks(results[0])
    query_grad = from_blocks(results[1])
    key_grad = from_blocks(results[2])
    value_grad = from_blocks(results[3])
    raw_mix = results[4].reshape(GROUPS, FILT)
    raw_skip = results[5].reshape(D)
    raw_feat = results[6].transpose(1, 2, 0, 3).reshape(3, SHORT, D)
    whole_sq = jnp.sum(raw_mix * raw_mix) + jnp.sum(raw_skip * raw_skip) + jnp.sum(raw_feat * raw_feat)
    total_params = GROUPS * FILT + D * (1 + 3 * SHORT)
    factor = lax.rsqrt(whole_sq / total_params + 1e-06)
    return (hyena_out, query_grad, key_grad, value_grad, raw_mix * factor, raw_skip * factor, raw_feat * factor)
```

```python
import jax
import jax.numpy as jnp
from jax import lax
from jax.experimental import pallas as pl
from jax.experimental.pallas import tpu as pltpu
from jax.sharding import PartitionSpec as P

F32 = jnp.float32
BF16 = jnp.bfloat16
I32 = jnp.int32
MESH = pl.DeviceIdType.MESH

NY = 4
HALO = 144
NEAR = 16
LANES = 128
SHORT = 7
FILT = 128
GROUP = 16
BIG = 1 << 28


def halo_kernel(nz, fill_ref, q_ref, k_ref, v_ref, g_ref, first_ref, from_prev, from_next,
                vbuf, tails, counts, load_sem, ysend, yrecv, zsend, zrecv, hsend, hrecv):
    me = lax.axis_index("ctx")
    z, y = me // NY, me % NY
    n = nz * NY
    nxt, prv = lax.rem(me + 1, n), lax.rem(me + n - 1, n)
    rows = q_ref.shape[0]

    loads = []
    for i, ref in enumerate((k_ref, v_ref, q_ref)):
        c = pltpu.make_async_copy(ref, vbuf.at[i], load_sem.at[i])
        c.start()
        loads.append(c)

    barrier = pltpu.get_barrier_semaphore()
    for d in range(1, NY):
        pl.semaphore_signal(barrier, inc=1, device_id={"ctx": z * NY + lax.rem(y + d, NY)}, device_id_type=MESH)
    for d in range(1, nz):
        pl.semaphore_signal(barrier, inc=1, device_id={"ctx": lax.rem(z + d, nz) * NY + y}, device_id_type=MESH)
    pl.semaphore_signal(barrier, inc=1, device_id={"ctx": nxt}, device_id_type=MESH)
    pl.semaphore_signal(barrier, inc=1, device_id={"ctx": prv}, device_id_type=MESH)
    fill = fill_ref[0]
    counts[z, y] = jnp.full((1, LANES), fill, I32)
    pl.semaphore_wait(barrier, NY - 1 + nz - 1 + 2)

    ycopies = []
    for d in range(1, NY):
        c = pltpu.make_async_remote_copy(
            src_ref=counts.at[z, y], dst_ref=counts.at[z, y], send_sem=ysend.at[d], recv_sem=yrecv.at[d],
            device_id={"ctx": z * NY + lax.rem(y + d, NY)}, device_id_type=MESH)
        c.start()
        ycopies.append(c)

    heads = []
    row = 0
    for i, (ref, count) in enumerate(((q_ref, HALO), (g_ref, HALO), (k_ref, NEAR), (v_ref, NEAR))):
        c = pltpu.make_async_remote_copy(
            src_ref=ref.at[pl.ds(0, count)], dst_ref=from_next.at[pl.ds(row, count)],
            send_sem=hsend.at[i], recv_sem=hrecv.at[i], device_id={"ctx": prv}, device_id_type=MESH)
        c.start()
        heads.append(c)
        row += count

    row = 0
    for i, count in enumerate((HALO, HALO, NEAR)):
        loads[i].wait()
        at = lax.broadcasted_iota(I32, (count, rows), 0) + (fill - count)
        pick = (at == lax.broadcasted_iota(I32, (count, rows), 1)).astype(BF16)
        tails[row:row + count, :] = jnp.dot(pick, vbuf[i], preferred_element_type=F32).astype(BF16)
        c = pltpu.make_async_remote_copy(
            src_ref=tails.at[pl.ds(row, count)], dst_ref=from_prev.at[pl.ds(row, count)],
            send_sem=hsend.at[4 + i], recv_sem=hrecv.at[4 + i], device_id={"ctx": nxt}, device_id_type=MESH)
        c.start()
        heads.append(c)
        row += count

    for c in ycopies:
        c.wait()
    zcopies = []
    for d in range(1, nz):
        c = pltpu.make_async_remote_copy(
            src_ref=counts.at[z], dst_ref=counts.at[z], send_sem=zsend.at[d], recv_sem=zrecv.at[d],
            device_id={"ctx": lax.rem(z + d, nz) * NY + y}, device_id_type=MESH)
        c.start()
        zcopies.append(c)
    for c in zcopies:
        c.wait()
    shard = (lax.broadcasted_iota(I32, counts.shape, 0) * NY + lax.broadcasted_iota(I32, counts.shape, 1))
    first_ref[...] = jnp.sum(jnp.where(shard < me, counts[...], 0), axis=(0, 1))
    for c in heads:
        c.wait()


def halo_call(nz, fill, q, k, v, g):
    rows, ch = q.shape
    return pl.pallas_call(
        lambda *refs: halo_kernel(nz, *refs),
        out_shape=(
            jax.ShapeDtypeStruct((1, LANES), I32),
            jax.ShapeDtypeStruct((2 * HALO + NEAR, ch), BF16),
            jax.ShapeDtypeStruct((2 * HALO + 2 * NEAR, ch), BF16),
        ),
        in_specs=[pl.BlockSpec(memory_space=pltpu.SMEM)] + [pl.BlockSpec(memory_space=pl.ANY)] * 4,
        out_specs=(
            pl.BlockSpec(memory_space=pltpu.VMEM),
            pl.BlockSpec(memory_space=pl.ANY),
            pl.BlockSpec(memory_space=pl.ANY),
        ),
        scratch_shapes=[
            pltpu.VMEM((3, rows, ch), BF16),
            pltpu.VMEM((2 * HALO + NEAR, ch), BF16),
            pltpu.VMEM((nz, NY, 1, LANES), I32),
            pltpu.SemaphoreType.DMA((3,)),
            pltpu.SemaphoreType.DMA((NY,)),
            pltpu.SemaphoreType.DMA((NY,)),
            pltpu.SemaphoreType.DMA((nz,)),
            pltpu.SemaphoreType.DMA((nz,)),
            pltpu.SemaphoreType.DMA((7,)),
            pltpu.SemaphoreType.DMA((7,)),
        ],
        compiler_params=pltpu.CompilerParams(collective_id=0, has_side_effects=True, vmem_limit_bytes=60 << 20),
        name="halo",
    )(fill, q, k, v, g)


OFF = HALO
QOFF = NEAR
OUT = 272
WIN = 400
MSLOT = 128


def mix_kernel(n, first_ref, fill_ref, docs_ref, q_ref, k_ref, v_ref, g_ref, hn_ref, hp_ref, ft_ref, taps_ref, skip_ref,
               ho_ref, qg_ref, kg_ref, vg_ref, pk_ref,
               qx, kx, vx, gw, query, keys, values, qb, kb, vb, m, gx, mown, dist, near, maskf, maskb, maskp, shift, taps):
    step = pl.program_id(0)
    rows = q_ref.shape[0]
    fill = fill_ref[0]
    last = lax.axis_index("ctx") == n - 1

    @pl.when(step == 0)
    def _():
        first = first_ref[0, 0]
        begins = [docs_ref[i] - first for i in range(docs_ref.shape[0])]
        end = jnp.where(last, fill, BIG)

        def doc_begin(slot):
            found = jnp.full(slot.shape, -BIG, I32)
            for b in begins:
                found = jnp.where(slot >= b, jnp.maximum(found, b), found)
            return found

        slot = lax.broadcasted_iota(I32, dist.shape, 0) - MSLOT
        dist[...] = slot - doc_begin(slot)
        slot = lax.broadcasted_iota(I32, near.shape, 0)
        until = jnp.full(slot.shape, BIG, I32)
        for b in begins:
            until = jnp.where(slot < b, jnp.minimum(until, b), until)
        near[...] = jnp.where(slot < fill, jnp.minimum(until, end) - 1 - slot, -1)
        for b, count in ((0, 128), (1, 128), (2, 16)):
            shape = (count, 256)
            a = lax.broadcasted_iota(I32, shape, 0)
            lane = lax.broadcasted_iota(I32, shape, 1)
            p, source = 128 * b + a, 128 * (b - 1) + lane
            j = p - source
            keep = (j >= 0) & (j < FILT) & (source >= doc_begin(p))
            maskf[128 * b:128 * b + count, :] = keep.astype(F32).astype(BF16)
            later = 128 * b + lane
            j = later - p
            begin = jnp.where(later < end, doc_begin(later), BIG)
            keep = (j >= 0) & (j < FILT) & (p >= begin)
            maskb[128 * b:128 * b + count, :] = keep.astype(F32).astype(BF16)
            if b < 2:
                p = 128 * b + 127 - a
                j = later - p
                maskp[128 * b:128 * b + count, :] = ((j >= 0) & (j < FILT) & (p >= begin)).astype(F32)
        r = lax.broadcasted_iota(I32, shift.shape, 0) + 192
        shift[...] = (r - fill == lax.broadcasted_iota(I32, shift.shape, 1)).astype(F32).astype(BF16)
        m[MSLOT + OUT:, :] = jnp.zeros((m.shape[0] - MSLOT - OUT, LANES), BF16)
        gx[WIN:, :] = jnp.zeros((gx.shape[0] - WIN, LANES), BF16)
        taps[...] = taps_ref[...].astype(F32)

    def own_or_next(ref, moved, begin, count):
        slot = lax.broadcasted_iota(I32, (count, LANES), 0) + begin
        return jnp.where(slot < fill, ref[begin:begin + count, :].astype(F32), moved)

    kx[0:OFF, :] = hn_ref[0:HALO, :].astype(F32)
    vx[0:OFF, :] = hn_ref[HALO:2 * HALO, :].astype(F32)
    qx[0:QOFF, :] = hn_ref[2 * HALO:2 * HALO + NEAR, :].astype(F32)
    moved_q = jnp.dot(shift[...], hp_ref[0:HALO, :], preferred_element_type=F32)
    moved_g = jnp.dot(shift[...], hp_ref[HALO:2 * HALO, :], preferred_element_type=F32)
    moved_k = jnp.dot(shift[0:80, 0:NEAR], hp_ref[2 * HALO:2 * HALO + NEAR, :], preferred_element_type=F32)
    moved_v = jnp.dot(shift[0:80, 0:NEAR], hp_ref[2 * HALO + NEAR:2 * HALO + 2 * NEAR, :], preferred_element_type=F32)
    for ref, out, off, moved in ((q_ref, qx, QOFF, moved_q), (g_ref, gw, 0, moved_g), (k_ref, kx, OFF, moved_k), (v_ref, vx, OFF, moved_v)):
        out[off:off + 192, :] = ref[0:192, :].astype(F32)
        out[off + 192:off + 256, :] = own_or_next(ref, moved[0:64], 192, 64)
        out[off + 256:off + 192 + moved.shape[0], :] = moved[64:]

    feat = [ft_ref[w].astype(F32) for w in range(3)]
    block = 16

    def featurize(window, at, far, w):
        acc = feat[w][0:1, :] * window[at:at + block, :]
        for j in range(1, SHORT):
            acc = acc + jnp.where(far >= j, feat[w][j:j + 1, :] * window[at - j:at - j + block, :], 0.0)
        return acc

    for s in range(-MSLOT, OUT, block):
        far = dist[s + MSLOT:s + MSLOT + block, :]
        key_rows = featurize(kx, OFF + s, far, 1)
        value_rows = featurize(vx, OFF + s, far, 2)
        m[MSLOT + s:MSLOT + s + block, :] = (key_rows * value_rows).astype(BF16)
        if s >= 0:
            keys[s:s + block, :] = key_rows
            values[s:s + block, :] = value_rows
    for s in range(0, WIN, block):
        far = dist[s + MSLOT:s + MSLOT + block, :]
        query_rows = featurize(qx, QOFF + s, far, 0)
        gx[s:s + block, :] = (query_rows * gw[s:s + block, :]).astype(BF16)
        if s < rows:
            query[s:s + block, :] = query_rows

    flip = (lax.broadcasted_iota(I32, (128, 128), 0) + lax.broadcasted_iota(I32, (128, 128), 1)) == 127
    for at in range(0, rows, 128):
        inside = lax.broadcasted_iota(I32, (128, 128), 1) + at < fill
        pick = jnp.where(flip & inside, 1.0, 0.0).astype(BF16)
        mown[at:at + 128, :] = jnp.dot(pick, m[MSLOT + at:MSLOT + at + 128, :], preferred_element_type=F32).astype(BF16)

    group_of = lax.broadcasted_iota(I32, (128, LANES), 1) // GROUP
    my_taps = taps[pl.ds(pl.multiple_of(step * 8, 8), 8), :]
    reverse = (lax.broadcasted_iota(I32, (FILT, FILT), 0) + lax.broadcasted_iota(I32, (FILT, FILT), 1)) % FILT == 0
    turned = jnp.dot(my_taps.astype(BF16), reverse.astype(F32).astype(BF16), preferred_element_type=F32)

    def circulant(row):
        return pltpu.roll(jnp.broadcast_to(row, (FILT, FILT)), 0, 1, stride=1, stride_axis=0)

    blocks = ((0, 128), (1, 128), (2, 16))
    skip = skip_ref[...]

    acc = [jnp.zeros((count, LANES), F32) for _, count in blocks]
    for g in range(8):
        circ = circulant(turned[g:g + 1, :]).astype(BF16)
        for b, count in blocks:
            both = jnp.concatenate([circ[:count], circ[:count]], axis=1) * maskf[128 * b:128 * b + count, :]
            res = jnp.dot(both, m[128 * b:128 * b + 256, :], preferred_element_type=F32)
            acc[b] = jnp.where(group_of[:count] == g, res, acc[b])
    for b, count in blocks:
        at = 128 * b
        gated = acc[b] + skip * m[MSLOT + at:MSLOT + at + count, :].astype(F32)
        qb[at:at + count, :] = (gw[at:at + count, :] * gated).astype(BF16).astype(F32)
        if b < 2:
            inside = lax.broadcasted_iota(I32, (count, LANES), 0) + at < fill
            ho_ref[at:at + count, :] = jnp.where(inside, query[at:at + count, :] * gated, 0.0).astype(BF16)

    acc = [jnp.zeros((count, LANES), F32) for _, count in blocks]
    mix_rows = []
    for g in range(8):
        circ = circulant(my_taps[g:g + 1, :]).astype(BF16)
        fold = jnp.zeros((128, FILT), F32)
        for b, count in blocks:
            both = jnp.concatenate([circ[:count], circ[:count]], axis=1) * maskb[128 * b:128 * b + count, :]
            window = gx[128 * b:128 * b + 256, :]
            res = jnp.dot(both, window, preferred_element_type=F32)
            acc[b] = jnp.where(group_of[:count] == g, res, acc[b])
            if b < 2:
                mine = jnp.where(group_of == g, mown[128 * b:128 * b + 128, :], jnp.zeros((), BF16))
                prod = lax.dot_general(mine, window, (((1,), (1,)), ((), ())), preferred_element_type=F32)
                prod = prod * maskp[128 * b:128 * b + 128, :]
                fold = fold + prod[:, :128] + prod[:, 128:]
        turned_back = pltpu.roll(fold, 1, 1, stride=1, stride_axis=0)
        mix_rows.append(jnp.sum(turned_back, axis=0, keepdims=True))
    for b, count in blocks:
        at = 128 * b
        back = acc[b] + skip * gx[at:at + count, :].astype(F32)
        kb[at:at + count, :] = (back * values[at:at + count, :]).astype(BF16).astype(F32)
        vb[at:at + count, :] = (back * keys[at:at + count, :]).astype(BF16).astype(F32)

    slot = lax.broadcasted_iota(I32, (rows, LANES), 0)
    both = m[MSLOT:MSLOT + rows, :].astype(F32) * gx[0:rows, :].astype(F32)
    skip_row = jnp.sum(jnp.where(slot < fill, both, 0.0), axis=0, keepdims=True)
    feat_rows = []
    for w, (back, window, off, out) in enumerate(((qb, qx, QOFF, qg_ref), (kb, kx, OFF, kg_ref), (vb, vx, OFF, vg_ref))):
        sums = [jnp.zeros((block, LANES), F32) for _ in range(SHORT)]
        for s in range(0, rows, block):
            reach = near[s:s + block, :]
            source = window[off + s:off + s + block, :]
            total = jnp.zeros((block, LANES), F32)
            for j in range(SHORT):
                later = jnp.where(reach >= j, back[s + j:s + j + block, :], 0.0)
                total = total + feat[w][j:j + 1, :] * later
                sums[j] = sums[j] + source * later
            out[s:s + block, :] = total.astype(BF16)
        feat_rows += [jnp.sum(x, axis=0, keepdims=True) for x in sums]
    packed = jnp.concatenate(mix_rows + [skip_row] + feat_rows + [jnp.zeros((2, LANES), F32)], axis=0)
    for i in range(8):
        pk_ref[i] = packed[4 * i:4 * i + 4, :]


def mix_call(n, first, fill, docs, q, k, v, g, hn, hp, ft, taps, skip):
    rows, ch = q.shape
    steps = ch // LANES
    col = lambda count: pl.BlockSpec((count, LANES), lambda i: (0, i))
    smem = pl.BlockSpec(memory_space=pltpu.SMEM)
    return pl.pallas_call(
        lambda *refs: mix_kernel(n, *refs),
        grid=(steps,),
        out_shape=tuple(jax.ShapeDtypeStruct((rows, ch), BF16) for _ in range(4))
        + (jax.ShapeDtypeStruct((8 * steps, 4, LANES), F32),),
        in_specs=[smem, smem, smem, col(rows), col(rows), col(rows), col(rows), col(hn.shape[0]), col(hp.shape[0]),
                  pl.BlockSpec((3, SHORT, LANES), lambda i: (0, 0, i)), pl.BlockSpec(taps.shape, lambda i: (0, 0)), col(1)],
        out_specs=(col(rows), col(rows), col(rows), col(rows), pl.BlockSpec((8, 4, LANES), lambda i: (i, 0, 0))),
        scratch_shapes=[
            pltpu.VMEM((QOFF + WIN, LANES), F32),
            pltpu.VMEM((OFF + OUT, LANES), F32),
            pltpu.VMEM((OFF + OUT, LANES), F32),
            pltpu.VMEM((WIN, LANES), F32),
            pltpu.VMEM((rows, LANES), F32),
            pltpu.VMEM((OUT, LANES), F32),
            pltpu.VMEM((OUT, LANES), F32),
            pltpu.VMEM((OUT, LANES), F32),
            pltpu.VMEM((OUT, LANES), F32),
            pltpu.VMEM((OUT, LANES), F32),
            pltpu.VMEM((512, LANES), BF16),
            pltpu.VMEM((512, LANES), BF16),
            pltpu.VMEM((rows, LANES), BF16),
            pltpu.VMEM((MSLOT + WIN, LANES), I32),
            pltpu.VMEM((rows, LANES), I32),
            pltpu.VMEM((OUT, 256), BF16),
            pltpu.VMEM((OUT, 256), BF16),
            pltpu.VMEM((rows, 256), F32),
            pltpu.VMEM((WIN - 192, HALO), BF16),
            pltpu.VMEM(taps.shape, F32),
        ],
        compiler_params=pltpu.CompilerParams(vmem_limit_bytes=60 << 20),
        name="mix",
    )(first, fill, docs, q, k, v, g, hn, hp, ft, taps, skip)


def sum_kernel(nz, ntp, params, pk_ref, mix_ref, skip_ref, feat_ref,
               got_y, part, got_z, full, squares, s1, r1, s2, r2, s3, r3, s4, r4, s5, r5):
    me = lax.axis_index("ctx")
    tp = lax.axis_index("tp")
    z, y = me // NY, me % NY

    def across_y(d):
        return {"ctx": z * NY + lax.rem(y + d, NY)}

    def across_z(d):
        return {"ctx": lax.rem(z + d, nz) * NY + y}

    def plane(e):
        dy, dt = e // ntp, e % ntp
        return {"ctx": z * NY + lax.rem(y + dy, NY), "tp": lax.rem(tp + dt, ntp)}

    barrier = pltpu.get_barrier_semaphore()
    for d in range(1, nz):
        pl.semaphore_signal(barrier, inc=1, device_id=across_z(d), device_id_type=MESH)
    for e in range(1, NY * ntp):
        pl.semaphore_signal(barrier, inc=1, device_id=plane(e), device_id_type=MESH)
    pl.semaphore_wait(barrier, nz - 1 + NY * ntp - 1)

    def send(src, dst, ssem, rsem, device):
        c = pltpu.make_async_remote_copy(src_ref=src, dst_ref=dst, send_sem=ssem, recv_sem=rsem,
                                         device_id=device, device_id_type=MESH)
        c.start()
        return c

    copies = [send(pk_ref.at[pl.ds(lax.rem(y + d, NY) * nz, nz)], got_y.at[d], s1.at[d], r1.at[d], across_y(d))
              for d in range(1, NY)]
    for c in copies:
        c.wait()
    total = pk_ref[pl.ds(y * nz, nz)]
    for d in range(1, NY):
        total = total + got_y[d]
    part[...] = total
    copies = [send(part.at[lax.rem(z + d, nz)], got_z.at[d], s2.at[d], r2.at[d], across_z(d)) for d in range(1, nz)]
    for c in copies:
        c.wait()
    piece = part[z]
    for d in range(1, nz):
        piece = piece + got_z[d]
    full[y * nz + z] = piece
    copies = [send(full.at[y * nz + z], full.at[y * nz + z], s3.at[d], r3.at[d], across_z(d)) for d in range(1, nz)]
    for c in copies:
        c.wait()
    mine = pl.ds(y * nz, nz)
    copies = [send(full.at[mine], full.at[mine], s4.at[d], r4.at[d], across_y(d)) for d in range(1, NY)]
    own = full[mine]
    square = jnp.sum(jnp.sum(own * own, axis=0), axis=0, keepdims=True)
    squares[y, tp] = jnp.broadcast_to(jnp.sum(square, axis=1, keepdims=True), (1, LANES))
    copies += [send(squares.at[y, tp], squares.at[y, tp], s5.at[e], r5.at[e], plane(e)) for e in range(1, NY * ntp)]
    for c in copies:
        c.wait()
    whole = jnp.sum(squares[...], axis=(0, 1))
    factor = lax.rsqrt(whole / params + 1e-06)
    for k in range(full.shape[0] // 8):
        mix_ref[8 * k:8 * k + 4, :] = full[8 * k] * factor
        mix_ref[8 * k + 4:8 * k + 8, :] = full[8 * k + 1] * factor
        lanes = slice(LANES * k, LANES * k + LANES)
        skip_ref[:, lanes] = full[8 * k + 2, 0:1] * factor
        for i in range(3 * SHORT):
            r = 9 + i
            feat_ref[i // SHORT, i % SHORT:i % SHORT + 1, lanes] = full[8 * k + r // 4, r % 4:r % 4 + 1] * factor


def sum_call(nz, ntp, params, pk, groups, ch):
    vmem = pl.BlockSpec(memory_space=pltpu.VMEM)
    dma = pltpu.SemaphoreType.DMA
    return pl.pallas_call(
        lambda *refs: sum_kernel(nz, ntp, params, *refs),
        out_shape=(
            jax.ShapeDtypeStruct((groups, FILT), F32),
            jax.ShapeDtypeStruct((1, ch), F32),
            jax.ShapeDtypeStruct((3, SHORT, ch), F32),
        ),
        in_specs=[vmem],
        out_specs=(vmem, vmem, vmem),
        scratch_shapes=[
            pltpu.VMEM((NY, nz, 4, LANES), F32),
            pltpu.VMEM((nz, 4, LANES), F32),
            pltpu.VMEM((nz, 4, LANES), F32),
            pltpu.VMEM((NY * nz, 4, LANES), F32),
            pltpu.VMEM((NY, ntp, 1, LANES), F32),
            dma((NY,)), dma((NY,)), dma((nz,)), dma((nz,)), dma((nz,)), dma((nz,)), dma((NY,)), dma((NY,)),
            dma((NY * ntp,)), dma((NY * ntp,)),
        ],
        compiler_params=pltpu.CompilerParams(collective_id=1, has_side_effects=True, vmem_limit_bytes=60 << 20),
        name="total",
    )(pk)


def solution(mesh):
    n, ntp = mesh.shape["ctx"], mesh.shape["tp"]
    nz = n // NY

    def shards(q, k, v, g, fill, docs, ft, taps, skip):
        groups, ch = taps.shape[0], q.shape[1]
        params = (groups * FILT + ch * (1 + 3 * SHORT)) * ntp
        first, hn, hp = halo_call(nz, fill, q, k, v, g)
        ho, qg, kg, vg, pk = mix_call(n, first, fill, docs, q, k, v, g, hn, hp, ft, taps, skip.reshape(1, ch))
        mix_grad, skip_grad, feat_grad = sum_call(nz, ntp, params, pk, groups, ch)
        return ho, qg, kg, vg, mix_grad, skip_grad.reshape(ch), feat_grad

    rows, whole = P("ctx", "tp"), P(None, None, "tp")
    return jax.shard_map(
        shards, mesh=mesh,
        in_specs=(rows, rows, rows, rows, P("ctx"), P(), whole, P("tp", None), P("tp")),
        out_specs=(rows, rows, rows, rows, P("tp", None), P("tp"), whole),
        check_vma=False)
```

```python
import jax
import jax.numpy as jnp
from jax import lax
from jax.experimental import pallas as pl
from jax.experimental.pallas import tpu as pltpu
from jax.sharding import PartitionSpec as P

F32 = jnp.float32
BF16 = jnp.bfloat16
I32 = jnp.int32
MESH = pl.DeviceIdType.MESH

NY = 4
HALO = 144
NEAR = 16
LANES = 128
SHORT = 7
FILT = 128
GROUP = 16
BIG = 1 << 28

OFF = HALO
QOFF = NEAR
OUT = 272
WIN = 400
MSLOT = 128

NEAREST = 16
NZB = 4


def mesh_copy(src, dst, ssem, rsem, device):
    c = pltpu.make_async_remote_copy(src_ref=src, dst_ref=dst, send_sem=ssem, recv_sem=rsem,
                                     device_id=device, device_id_type=MESH)
    c.start()
    return c


class Peers:
    def __init__(self, nz, ntp):
        self.nz, self.ntp = nz, ntp
        self.me = lax.axis_index("ctx")
        self.tp = lax.axis_index("tp")
        self.z, self.y = self.me // NY, self.me % NY
        self.za, self.zb = self.z // NZB, self.z % NZB
        self.nza = nz // NZB

    def along_y(self, d):
        return {"ctx": self.z * NY + lax.rem(self.y + d, NY)}

    def along_z(self, d):
        return {"ctx": lax.rem(self.z + d, self.nz) * NY + self.y}

    def step(self, d):
        return {"ctx": lax.rem(self.me + d + self.nz * NY, self.nz * NY)}

    def near(self, e):
        y, zb = lax.rem(self.y + e // NZB, NY), lax.rem(self.zb + e % NZB, NZB)
        return y * NZB + zb, {"ctx": (self.za * NZB + zb) * NY + y}

    def far(self, d):
        return {"ctx": (lax.rem(self.za + d, self.nza) * NZB + self.zb) * NY + self.y}

    def along_tp(self, d):
        return {"tp": lax.rem(self.tp + d, self.ntp)}


def exchange(at, fill, q_ref, k_ref, v_ref, g_ref, first, hn, hp, vbuf, tails, counts,
             load_sem, ysend, yrecv, zsend, zrecv, hsend, hrecv):
    nz, rows = at.nz, q_ref.shape[0]
    loads = []
    for i, ref in enumerate((k_ref, v_ref, q_ref)):
        c = pltpu.make_async_copy(ref, vbuf.at[i], load_sem.at[i])
        c.start()
        loads.append(c)

    barrier = pltpu.get_barrier_semaphore()
    partners = [at.along_y(d) for d in range(1, NY)] + [at.along_z(d) for d in range(1, nz)] + [at.step(1), at.step(-1)]
    partners += [at.near(e)[1] for e in range(1, NEAREST)] + [at.along_tp(d) for d in range(1, at.ntp)]
    for device in partners:
        pl.semaphore_signal(barrier, inc=1, device_id=device, device_id_type=MESH)
    counts[at.z, at.y] = jnp.full((1, LANES), fill, I32)
    pl.semaphore_wait(barrier, len(partners))

    own = counts.at[at.z, at.y]
    ycopies = [mesh_copy(own, own, ysend.at[d], yrecv.at[d], at.along_y(d)) for d in range(1, NY)]
    copies = []
    row = 0
    for i, (ref, count) in enumerate(((q_ref, HALO), (g_ref, HALO), (k_ref, NEAR), (v_ref, NEAR))):
        copies.append(mesh_copy(ref.at[pl.ds(0, count)], hp.at[pl.ds(row, count)], hsend.at[i], hrecv.at[i], at.step(-1)))
        row += count
    row = 0
    for i, count in enumerate((HALO, HALO, NEAR)):
        loads[i].wait()
        slot = lax.broadcasted_iota(I32, (count, rows), 0) + (fill - count)
        pick = (slot == lax.broadcasted_iota(I32, (count, rows), 1)).astype(F32).astype(BF16)
        tails[row:row + count, :] = jnp.dot(pick, vbuf[i], preferred_element_type=F32).astype(BF16)
        part = pl.ds(row, count)
        copies.append(mesh_copy(tails.at[part], hn.at[part], hsend.at[4 + i], hrecv.at[4 + i], at.step(1)))
        row += count
    for c in ycopies:
        c.wait()
    own = counts.at[at.z]
    zcopies = [mesh_copy(own, own, zsend.at[d], zrecv.at[d], at.along_z(d)) for d in range(1, nz)]
    for c in zcopies:
        c.wait()
    shard = lax.broadcasted_iota(I32, counts.shape, 0) * NY + lax.broadcasted_iota(I32, counts.shape, 1)
    first[...] = jnp.sum(jnp.where(shard < at.me, counts[...], 0), axis=(0, 1))
    for c in copies:
        c.wait()


def sum_shards(at, params, raw, got, parts, full, squares, s1, r1, s2, r2, s3, r3, s4, r4, out_ref):
    mine = at.y * NZB + at.zb
    copies = []
    for e in range(1, NEAREST):
        piece, device = at.near(e)
        copies.append(mesh_copy(raw.at[piece], got.at[e], s1.at[e], r1.at[e], device))
    for c in copies:
        c.wait()
    acc = raw[mine]
    for e in range(1, NEAREST):
        acc = acc + got[e]
    parts[at.za] = acc
    own = parts.at[at.za]
    copies = [mesh_copy(own, own, s2.at[d], r2.at[d], at.far(d)) for d in range(1, at.nza)]
    for c in copies:
        c.wait()
    acc = parts[0]
    for d in range(1, at.nza):
        acc = acc + parts[d]
    full[mine] = acc
    own = full.at[mine]
    copies = [mesh_copy(own, own, s3.at[e], r3.at[e], at.near(e)[1]) for e in range(1, NEAREST)]
    for c in copies:
        c.wait()
    square = jnp.zeros(full.shape[1:], F32)
    for i in range(NEAREST):
        square = square + full[i] * full[i]
    square = jnp.sum(jnp.sum(square, axis=0, keepdims=True), axis=1, keepdims=True)
    squares[at.tp] = jnp.broadcast_to(square, (1, LANES))
    own = squares.at[at.tp]
    copies = [mesh_copy(own, own, s4.at[d], r4.at[d], at.along_tp(d)) for d in range(1, at.ntp)]
    for c in copies:
        c.wait()
    factor = lax.rsqrt(jnp.sum(squares[...], axis=0) / params + 1e-06)
    for i in range(NEAREST):
        out_ref[i] = full[i] * factor


def mix_kernel(nz, ntp, params, fill_ref, docs_ref, qw_ref, kw_ref, vw_ref, gw_ref, q_ref, k_ref, v_ref, g_ref, ft_ref, taps_ref, skip_ref,
               ho_ref, qg_ref, kg_ref, vg_ref, pk_ref,
               qx, kx, vx, gw, query, keys, values, qb, kb, vb, m, gx, mown, dist, near, maskf, maskb, maskp, shift, taps,
               first_row, hn, hp, vbuf, tails, counts, raw, got, parts, full, squares,
               load_sem, ysend, yrecv, zsend, zrecv, hsend, hrecv, s1, r1, s2, r2, s3, r3, s4, r4):
    step = pl.program_id(0)
    rows = q_ref.shape[0]
    fill = fill_ref[0]
    peers = Peers(nz, ntp)
    last = peers.me == nz * NY - 1

    @pl.when(step == 0)
    def _():
        exchange(peers, fill, qw_ref, kw_ref, vw_ref, gw_ref, first_row, hn, hp, vbuf, tails, counts,
                 load_sem, ysend, yrecv, zsend, zrecv, hsend, hrecv)
        begin_rows = [docs_ref[i] - first_row[...] for i in range(docs_ref.shape[0])]
        end = jnp.where(last, fill, BIG)

        def doc_begin(slot):
            found = jnp.full(slot.shape, -BIG, I32)
            for b in begin_rows:
                b = jnp.broadcast_to(b[:, 0:1], slot.shape)
                found = jnp.where(slot >= b, jnp.maximum(found, b), found)
            return found

        slot = lax.broadcasted_iota(I32, dist.shape, 0) - MSLOT
        dist[...] = slot - doc_begin(slot)
        slot = lax.broadcasted_iota(I32, near.shape, 0)
        until = jnp.full(slot.shape, BIG, I32)
        for b in begin_rows:
            b = jnp.broadcast_to(b[:, 0:1], slot.shape)
            until = jnp.where(slot < b, jnp.minimum(until, b), until)
        near[...] = jnp.where(slot < fill, jnp.minimum(until, end) - 1 - slot, -1)
        for b, count in ((0, 128), (1, 128), (2, 16)):
            shape = (count, 256)
            a = lax.broadcasted_iota(I32, shape, 0)
            lane = lax.broadcasted_iota(I32, shape, 1)
            p, source = 128 * b + a, 128 * (b - 1) + lane
            j = p - source
            keep = (j >= 0) & (j < FILT) & (source >= doc_begin(p))
            maskf[128 * b:128 * b + count, :] = keep.astype(F32).astype(BF16)
            later = 128 * b + lane
            j = later - p
            begin = jnp.where(later < end, doc_begin(later), BIG)
            keep = (j >= 0) & (j < FILT) & (p >= begin)
            maskb[128 * b:128 * b + count, :] = keep.astype(F32).astype(BF16)
            if b < 2:
                p = 128 * b + 127 - a
                j = later - p
                maskp[128 * b:128 * b + count, :] = ((j >= 0) & (j < FILT) & (p >= begin)).astype(F32)
        r = lax.broadcasted_iota(I32, shift.shape, 0) + 192
        shift[...] = (r - fill == lax.broadcasted_iota(I32, shift.shape, 1)).astype(F32).astype(BF16)
        m[MSLOT + OUT:, :] = jnp.zeros((m.shape[0] - MSLOT - OUT, LANES), BF16)
        gx[WIN:, :] = jnp.zeros((gx.shape[0] - WIN, LANES), BF16)
        taps[...] = taps_ref[...].astype(F32)

    def own_or_next(ref, moved, begin, count):
        slot = lax.broadcasted_iota(I32, (count, LANES), 0) + begin
        return jnp.where(slot < fill, ref[begin:begin + count, :].astype(F32), moved)

    lanes = pl.ds(pl.multiple_of(step * LANES, LANES), LANES)
    kx[0:OFF, :] = hn[0:HALO, lanes].astype(F32)
    vx[0:OFF, :] = hn[HALO:2 * HALO, lanes].astype(F32)
    qx[0:QOFF, :] = hn[2 * HALO:2 * HALO + NEAR, lanes].astype(F32)
    moved_q = jnp.dot(shift[...], hp[0:HALO, lanes], preferred_element_type=F32)
    moved_g = jnp.dot(shift[...], hp[HALO:2 * HALO, lanes], preferred_element_type=F32)
    moved_k = jnp.dot(shift[0:80, 0:NEAR], hp[2 * HALO:2 * HALO + NEAR, lanes], preferred_element_type=F32)
    moved_v = jnp.dot(shift[0:80, 0:NEAR], hp[2 * HALO + NEAR:2 * HALO + 2 * NEAR, lanes], preferred_element_type=F32)
    for ref, out, off, moved in ((q_ref, qx, QOFF, moved_q), (g_ref, gw, 0, moved_g), (k_ref, kx, OFF, moved_k), (v_ref, vx, OFF, moved_v)):
        out[off:off + 192, :] = ref[0:192, :].astype(F32)
        out[off + 192:off + 256, :] = own_or_next(ref, moved[0:64], 192, 64)
        out[off + 256:off + 192 + moved.shape[0], :] = moved[64:]

    feat = [ft_ref[w].astype(F32) for w in range(3)]
    block = 16

    def featurize(window, at, far, w):
        acc = feat[w][0:1, :] * window[at:at + block, :]
        for j in range(1, SHORT):
            acc = acc + jnp.where(far >= j, feat[w][j:j + 1, :] * window[at - j:at - j + block, :], 0.0)
        return acc

    for s in range(-MSLOT, OUT, block):
        far = dist[s + MSLOT:s + MSLOT + block, :]
        key_rows = featurize(kx, OFF + s, far, 1)
        value_rows = featurize(vx, OFF + s, far, 2)
        m[MSLOT + s:MSLOT + s + block, :] = (key_rows * value_rows).astype(BF16)
        if s >= 0:
            keys[s:s + block, :] = key_rows
            values[s:s + block, :] = value_rows
    for s in range(0, WIN, block):
        far = dist[s + MSLOT:s + MSLOT + block, :]
        query_rows = featurize(qx, QOFF + s, far, 0)
        gx[s:s + block, :] = (query_rows * gw[s:s + block, :]).astype(BF16)
        if s < rows:
            query[s:s + block, :] = query_rows

    flip = (lax.broadcasted_iota(I32, (128, 128), 0) + lax.broadcasted_iota(I32, (128, 128), 1)) == 127
    for at in range(0, rows, 128):
        inside = lax.broadcasted_iota(I32, (128, 128), 1) + at < fill
        pick = jnp.where(flip & inside, 1.0, 0.0).astype(BF16)
        mown[at:at + 128, :] = jnp.dot(pick, m[MSLOT + at:MSLOT + at + 128, :], preferred_element_type=F32).astype(BF16)

    group_of = lax.broadcasted_iota(I32, (128, LANES), 1) // GROUP
    my_taps = taps[pl.ds(pl.multiple_of(step * 8, 8), 8), :]
    reverse = (lax.broadcasted_iota(I32, (FILT, FILT), 0) + lax.broadcasted_iota(I32, (FILT, FILT), 1)) % FILT == 0
    turned = jnp.dot(my_taps.astype(BF16), reverse.astype(F32).astype(BF16), preferred_element_type=F32)

    def circulant(row):
        return pltpu.roll(jnp.broadcast_to(row, (FILT, FILT)), 0, 1, stride=1, stride_axis=0)

    blocks = ((0, 128), (1, 128), (2, 16))
    skip = skip_ref[...]

    acc = [jnp.zeros((count, LANES), F32) for _, count in blocks]
    for g in range(8):
        circ = circulant(turned[g:g + 1, :]).astype(BF16)
        for b, count in blocks:
            both = jnp.concatenate([circ[:count], circ[:count]], axis=1) * maskf[128 * b:128 * b + count, :]
            res = jnp.dot(both, m[128 * b:128 * b + 256, :], preferred_element_type=F32)
            acc[b] = jnp.where(group_of[:count] == g, res, acc[b])
    for b, count in blocks:
        at = 128 * b
        gated = acc[b] + skip * m[MSLOT + at:MSLOT + at + count, :].astype(F32)
        qb[at:at + count, :] = (gw[at:at + count, :] * gated).astype(BF16).astype(F32)
        if b < 2:
            inside = lax.broadcasted_iota(I32, (count, LANES), 0) + at < fill
            ho_ref[at:at + count, :] = jnp.where(inside, query[at:at + count, :] * gated, 0.0).astype(BF16)

    acc = [jnp.zeros((count, LANES), F32) for _, count in blocks]
    mix_rows = []
    for g in range(8):
        circ = circulant(my_taps[g:g + 1, :]).astype(BF16)
        fold = jnp.zeros((128, FILT), F32)
        for b, count in blocks:
            both = jnp.concatenate([circ[:count], circ[:count]], axis=1) * maskb[128 * b:128 * b + count, :]
            window = gx[128 * b:128 * b + 256, :]
            res = jnp.dot(both, window, preferred_element_type=F32)
            acc[b] = jnp.where(group_of[:count] == g, res, acc[b])
            if b < 2:
                mine = jnp.where(group_of == g, mown[128 * b:128 * b + 128, :], jnp.zeros((), BF16))
                prod = lax.dot_general(mine, window, (((1,), (1,)), ((), ())), preferred_element_type=F32)
                prod = prod * maskp[128 * b:128 * b + 128, :]
                fold = fold + prod[:, :128] + prod[:, 128:]
        turned_back = pltpu.roll(fold, 1, 1, stride=1, stride_axis=0)
        mix_rows.append(jnp.sum(turned_back, axis=0, keepdims=True))
    for b, count in blocks:
        at = 128 * b
        back = acc[b] + skip * gx[at:at + count, :].astype(F32)
        kb[at:at + count, :] = (back * values[at:at + count, :]).astype(BF16).astype(F32)
        vb[at:at + count, :] = (back * keys[at:at + count, :]).astype(BF16).astype(F32)

    slot = lax.broadcasted_iota(I32, (rows, LANES), 0)
    both = m[MSLOT:MSLOT + rows, :].astype(F32) * gx[0:rows, :].astype(F32)
    skip_row = jnp.sum(jnp.where(slot < fill, both, 0.0), axis=0, keepdims=True)
    feat_rows = []
    for w, (back, window, off, out) in enumerate(((qb, qx, QOFF, qg_ref), (kb, kx, OFF, kg_ref), (vb, vx, OFF, vg_ref))):
        sums = [jnp.zeros((block, LANES), F32) for _ in range(SHORT)]
        for s in range(0, rows, block):
            reach = near[s:s + block, :]
            source = window[off + s:off + s + block, :]
            total = jnp.zeros((block, LANES), F32)
            for j in range(SHORT):
                later = jnp.where(reach >= j, back[s + j:s + j + block, :], 0.0)
                total = total + feat[w][j:j + 1, :] * later
                sums[j] = sums[j] + source * later
            out[s:s + block, :] = total.astype(BF16)
        feat_rows += [jnp.sum(x, axis=0, keepdims=True) for x in sums]
    packed = jnp.concatenate(mix_rows + [skip_row] + feat_rows + [jnp.zeros((2, LANES), F32)], axis=0)
    raw[2 * step] = packed[0:16]
    raw[2 * step + 1] = packed[16:32]

    @pl.when(step == pl.num_programs(0) - 1)
    def _():
        sum_shards(peers, params, raw, got, parts, full, squares, s1, r1, s2, r2, s3, r3, s4, r4, pk_ref)


def mix_call(nz, ntp, params, fill, docs, q, k, v, g, ft, taps, skip):
    rows, ch = q.shape
    steps = ch // LANES
    col = lambda count: pl.BlockSpec((count, LANES), lambda i: (0, i))
    smem = pl.BlockSpec(memory_space=pltpu.SMEM)
    hbm = pl.BlockSpec(memory_space=pl.ANY)
    dma = pltpu.SemaphoreType.DMA
    piece = (16, LANES)
    return pl.pallas_call(
        lambda *refs: mix_kernel(nz, ntp, params, *refs),
        grid=(steps,),
        out_shape=tuple(jax.ShapeDtypeStruct((rows, ch), BF16) for _ in range(4))
        + (jax.ShapeDtypeStruct((NEAREST, *piece), F32),),
        in_specs=[smem, smem, hbm, hbm, hbm, hbm, col(rows), col(rows), col(rows), col(rows),
                  pl.BlockSpec((3, SHORT, LANES), lambda i: (0, 0, i)), pl.BlockSpec(taps.shape, lambda i: (0, 0)), col(1)],
        out_specs=(col(rows), col(rows), col(rows), col(rows), pl.BlockSpec((NEAREST, *piece), lambda i: (0, 0, 0))),
        scratch_shapes=[
            pltpu.VMEM((QOFF + WIN, LANES), F32),
            pltpu.VMEM((OFF + OUT, LANES), F32),
            pltpu.VMEM((OFF + OUT, LANES), F32),
            pltpu.VMEM((WIN, LANES), F32),
            pltpu.VMEM((rows, LANES), F32),
            pltpu.VMEM((OUT, LANES), F32),
            pltpu.VMEM((OUT, LANES), F32),
            pltpu.VMEM((OUT, LANES), F32),
            pltpu.VMEM((OUT, LANES), F32),
            pltpu.VMEM((OUT, LANES), F32),
            pltpu.VMEM((512, LANES), BF16),
            pltpu.VMEM((512, LANES), BF16),
            pltpu.VMEM((rows, LANES), BF16),
            pltpu.VMEM((MSLOT + WIN, LANES), I32),
            pltpu.VMEM((rows, LANES), I32),
            pltpu.VMEM((OUT, 256), BF16),
            pltpu.VMEM((OUT, 256), BF16),
            pltpu.VMEM((rows, 256), F32),
            pltpu.VMEM((WIN - 192, HALO), BF16),
            pltpu.VMEM(taps.shape, F32),
            pltpu.VMEM((1, LANES), I32),
            pltpu.VMEM((2 * HALO + NEAR, ch), BF16),
            pltpu.VMEM((2 * HALO + 2 * NEAR, ch), BF16),
            pltpu.VMEM((3, rows, ch), BF16),
            pltpu.VMEM((2 * HALO + NEAR, ch), BF16),
            pltpu.VMEM((nz, NY, 1, LANES), I32),
            pltpu.VMEM((NEAREST, *piece), F32),
            pltpu.VMEM((NEAREST, *piece), F32),
            pltpu.VMEM((nz // NZB, *piece), F32),
            pltpu.VMEM((NEAREST, *piece), F32),
            pltpu.VMEM((ntp, 1, LANES), F32),
            dma((3,)), dma((NY,)), dma((NY,)), dma((nz,)), dma((nz,)), dma((7,)), dma((7,)),
            dma((NEAREST,)), dma((NEAREST,)), dma((nz // NZB,)), dma((nz // NZB,)), dma((NEAREST,)), dma((NEAREST,)),
            dma((ntp,)), dma((ntp,)),
        ],
        compiler_params=pltpu.CompilerParams(collective_id=0, has_side_effects=True, vmem_limit_bytes=60 << 20),
        name="mix",
    )(fill, docs, q, k, v, g, q, k, v, g, ft, taps, skip)


def place_kernel(*refs):
    pk_ref, mix_ref, skip_ref, feat_ref = refs[4], *refs[9:]
    for source, out in zip(refs[:4], refs[5:9]):
        out[...] = source[...]

    @pl.when(pl.program_id(0) == 0)
    def _():
        for k in range(pk_ref.shape[0] // 2):
            lanes = slice(LANES * k, LANES * k + LANES)
            mix_ref[8 * k:8 * k + 8, :] = pk_ref[2 * k, 0:8]
            skip_ref[:, lanes] = pk_ref[2 * k, 8:9]
            for w in range(3):
                for j in range(SHORT):
                    r = 9 + SHORT * w + j
                    feat_ref[w, j:j + 1, lanes] = pk_ref[2 * k + r // 16, r % 16:r % 16 + 1]


def place_call(big, pk, groups):
    rows, ch = big[0].shape
    whole = lambda *shape: pl.BlockSpec(shape, lambda i: (0,) * len(shape))
    part = pl.BlockSpec((64, ch), lambda i: (i, 0))
    return pl.pallas_call(
        place_kernel,
        grid=(rows // 64,),
        out_shape=tuple(jax.ShapeDtypeStruct((rows, ch), BF16) for _ in range(4)) + (
            jax.ShapeDtypeStruct((groups, FILT), F32),
            jax.ShapeDtypeStruct((1, ch), F32),
            jax.ShapeDtypeStruct((3, SHORT, ch), F32),
        ),
        in_specs=[part] * 4 + [whole(*pk.shape)],
        out_specs=(part,) * 4 + (whole(groups, FILT), whole(1, ch), whole(3, SHORT, ch)),
        compiler_params=pltpu.CompilerParams(vmem_limit_bytes=60 << 20),
        name="place",
    )(*big, pk)


def solution(mesh):
    n, ntp = mesh.shape["ctx"], mesh.shape["tp"]
    nz = n // NY

    def shards(q, k, v, g, fill, docs, ft, taps, skip):
        groups, ch = taps.shape[0], q.shape[1]
        params = (groups * FILT + ch * (1 + 3 * SHORT)) * ntp
        *big, pk = mix_call(nz, ntp, params, fill, docs, q, k, v, g, ft, taps, skip.reshape(1, ch))
        *big, mix_grad, skip_grad, feat_grad = place_call(big, pk, groups)
        return *big, mix_grad, skip_grad.reshape(ch), feat_grad

    rows, whole = P("ctx", "tp"), P(None, None, "tp")
    return jax.shard_map(
        shards, mesh=mesh,
        in_specs=(rows, rows, rows, rows, P("ctx"), P(), whole, P("tp", None), P("tp")),
        out_specs=(rows, rows, rows, rows, P("tp", None), P("tp"), whole),
        check_vma=False)
```

```python
import jax
import jax.numpy as jnp
from jax import lax
from jax.experimental import pallas as pl
from jax.experimental.pallas import tpu as pltpu
from jax.sharding import PartitionSpec as P

F32 = jnp.float32
BF16 = jnp.bfloat16
I32 = jnp.int32
MESH = pl.DeviceIdType.MESH

NY = 4
HALO = 144
NEAR = 16
LANES = 128
SHORT = 7
FILT = 128
GROUP = 16
BIG = 1 << 28

OFF = HALO
QOFF = NEAR
OUT = 272
WIN = 400
MSLOT = 128

NEAREST = 16
NZB = 4
PARTS = ((0, 1), (1, 3), (3, 8))
TAILS = (HALO, HALO, NEAR)


def mesh_copy(src, dst, ssem, rsem, device):
    c = pltpu.make_async_remote_copy(src_ref=src, dst_ref=dst, send_sem=ssem, recv_sem=rsem,
                                     device_id=device, device_id_type=MESH)
    c.start()
    return c


def piece_copy(raw, got, s1, r1, piece, e, device):
    return pltpu.make_async_remote_copy(src_ref=raw.at[piece], dst_ref=got.at[e], send_sem=s1.at[e], recv_sem=r1.at[e],
                                        device_id=device, device_id_type=MESH)


class Peers:
    def __init__(self, nz, ntp):
        self.nz, self.ntp = nz, ntp
        self.me = lax.axis_index("ctx")
        self.tp = lax.axis_index("tp")
        self.z, self.y = self.me // NY, self.me % NY
        self.za, self.zb = self.z // NZB, self.z % NZB
        self.nza = nz // NZB

    def along_y(self, d):
        return {"ctx": self.z * NY + lax.rem(self.y + d, NY)}

    def along_z(self, d):
        return {"ctx": lax.rem(self.z + d, self.nz) * NY + self.y}

    def step(self, d):
        return {"ctx": lax.rem(self.me + d + self.nz * NY, self.nz * NY)}

    def near(self, e):
        y, zb = lax.rem(self.y + e // NZB, NY), lax.rem(self.zb + e % NZB, NZB)
        return y * NZB + zb, {"ctx": (self.za * NZB + zb) * NY + y}

    def far(self, d):
        return {"ctx": (lax.rem(self.za + d, self.nza) * NZB + self.zb) * NY + self.y}

    def owner(self, piece):
        y, zb = piece // NZB, piece % NZB
        e = lax.rem(y - self.y + NY, NY) * NZB + lax.rem(zb - self.zb + NZB, NZB)
        return e, {"ctx": (self.za * NZB + zb) * NY + y}

    def other_core(self):
        return {"tp": self.tp + 1 - 2 * (self.tp % 2)}

    def along_x(self, d):
        return {"tp": lax.rem(self.tp + 2 * d, self.ntp)}


def exchange(at, fill, q_ref, k_ref, v_ref, g_ref, first, hn, hp, vbuf, tails, counts,
             load_sem, ysend, yrecv, zsend, zrecv, hsend, hrecv):
    nz, rows = at.nz, q_ref.shape[0]
    loads = []
    for i, ref in enumerate((k_ref, v_ref, q_ref)):
        c = pltpu.make_async_copy(ref, vbuf.at[i], load_sem.at[i])
        c.start()
        loads.append(c)

    barrier = pltpu.get_barrier_semaphore()
    partners = [at.along_y(d) for d in range(1, NY)] + [at.along_z(d) for d in range(1, nz)] + [at.step(1), at.step(-1)]
    partners += [at.near(e)[1] for e in range(1, NEAREST)] + [at.other_core()] + [at.along_x(d) for d in range(1, at.ntp // 2)]
    for device in partners:
        pl.semaphore_signal(barrier, inc=1, device_id=device, device_id_type=MESH)
    counts[at.z, at.y] = jnp.full((1, LANES), fill, I32)
    pl.semaphore_wait(barrier, len(partners))

    own = counts.at[at.z, at.y]
    ycopies = [mesh_copy(own, own, ysend.at[d], yrecv.at[d], at.along_y(d)) for d in range(1, NY)]
    for part in range(len(PARTS)):
        for c in head_copies(at, part, q_ref, k_ref, v_ref, g_ref, hp, hsend, hrecv):
            c.start()
        row = 0
        for i, count in enumerate(TAILS):
            if part == 0:
                loads[i].wait()
                slot = lax.broadcasted_iota(I32, (count, rows), 0) + (fill - count)
                pick = (slot == lax.broadcasted_iota(I32, (count, rows), 1)).astype(F32).astype(BF16)
                tails[row:row + count, :] = jnp.dot(pick, vbuf[i], preferred_element_type=F32).astype(BF16)
            row += count
        for c in tail_copies(at, part, tails, hn, hsend, hrecv):
            c.start()
    for c in ycopies:
        c.wait()
    own = counts.at[at.z]
    zcopies = [mesh_copy(own, own, zsend.at[d], zrecv.at[d], at.along_z(d)) for d in range(1, nz)]
    for c in zcopies:
        c.wait()
    shard = lax.broadcasted_iota(I32, counts.shape, 0) * NY + lax.broadcasted_iota(I32, counts.shape, 1)
    first[...] = jnp.sum(jnp.where(shard < at.me, counts[...], 0), axis=(0, 1))


def head_copies(at, part, q_ref, k_ref, v_ref, g_ref, hp, hsend, hrecv):
    copies, row = [], 0
    cols = pl.ds(PARTS[part][0] * LANES, (PARTS[part][1] - PARTS[part][0]) * LANES)
    for i, (ref, count) in enumerate(((q_ref, HALO), (g_ref, HALO), (k_ref, NEAR), (v_ref, NEAR))):
        copies.append(pltpu.make_async_remote_copy(
            src_ref=ref.at[pl.ds(0, count), cols], dst_ref=hp.at[pl.ds(row, count), cols],
            send_sem=hsend.at[part, i], recv_sem=hrecv.at[part, i], device_id=at.step(-1), device_id_type=MESH))
        row += count
    return copies


def tail_copies(at, part, tails, hn, hsend, hrecv):
    copies, row = [], 0
    cols = pl.ds(PARTS[part][0] * LANES, (PARTS[part][1] - PARTS[part][0]) * LANES)
    for i, count in enumerate(TAILS):
        rows = pl.ds(row, count)
        copies.append(pltpu.make_async_remote_copy(
            src_ref=tails.at[rows, cols], dst_ref=hn.at[rows, cols],
            send_sem=hsend.at[part, 4 + i], recv_sem=hrecv.at[part, 4 + i], device_id=at.step(1), device_id_type=MESH))
        row += count
    return copies


def sum_shards(at, params, raw, got, parts, full, squares, s1, r1, s2, r2, s3, r3, s4, r4, out_ref):
    mine = at.y * NZB + at.zb
    for e in range(1, NEAREST):
        piece, device = at.near(e)
        piece_copy(raw, got, s1, r1, piece, e, device).wait()
    acc = raw[mine]
    for e in range(1, NEAREST):
        acc = acc + got[e]
    parts[at.za] = acc
    own = parts.at[at.za]
    copies = [mesh_copy(own, own, s2.at[d], r2.at[d], at.far(d)) for d in range(1, at.nza)]
    for c in copies:
        c.wait()
    acc = parts[0]
    for d in range(1, at.nza):
        acc = acc + parts[d]
    full[mine] = acc
    own = full.at[mine]
    copies = [mesh_copy(own, own, s3.at[e], r3.at[e], at.near(e)[1]) for e in range(1, NEAREST)]
    for c in copies:
        c.wait()
    square = jnp.zeros(full.shape[1:], F32)
    for i in range(NEAREST):
        square = square + full[i] * full[i]
    square = jnp.sum(jnp.sum(square, axis=0, keepdims=True), axis=1, keepdims=True)
    chip, core = at.tp // 2, at.tp % 2
    squares[chip, core] = jnp.broadcast_to(square, (1, LANES))
    own = squares.at[chip, core]
    mesh_copy(own, own, s4.at[0], r4.at[0], at.other_core()).wait()
    own = squares.at[chip]
    copies = [mesh_copy(own, own, s4.at[d], r4.at[d], at.along_x(d)) for d in range(1, at.ntp // 2)]
    for c in copies:
        c.wait()
    factor = lax.rsqrt(jnp.sum(squares[...], axis=(0, 1)) / params + 1e-06)
    for i in range(NEAREST):
        out_ref[i] = full[i] * factor


def mix_kernel(nz, ntp, params, fill_ref, docs_ref, qw_ref, kw_ref, vw_ref, gw_ref, q_ref, k_ref, v_ref, g_ref, ft_ref, taps_ref, skip_ref,
               ho_ref, qg_ref, kg_ref, vg_ref, pk_ref,
               qx, kx, vx, gw, query, keys, values, qb, kb, vb, m, gx, mown, dist, near, maskf, maskb, maskp, shift, taps, qo, ko, vo,
               first_row, hn, hp, vbuf, tails, counts, raw, got, parts, full, squares,
               load_sem, ysend, yrecv, zsend, zrecv, hsend, hrecv, s1, r1, s2, r2, s3, r3, s4, r4):
    step = pl.program_id(0)
    rows = q_ref.shape[0]
    fill = fill_ref[0]
    peers = Peers(nz, ntp)
    last = peers.me == nz * NY - 1

    @pl.when(step == 0)
    def _():
        exchange(peers, fill, qw_ref, kw_ref, vw_ref, gw_ref, first_row, hn, hp, vbuf, tails, counts,
                 load_sem, ysend, yrecv, zsend, zrecv, hsend, hrecv)
        begin_rows = [docs_ref[i] - first_row[...] for i in range(docs_ref.shape[0])]
        end = jnp.where(last, fill, BIG)

        def doc_begin(slot):
            found = jnp.full(slot.shape, -BIG, I32)
            for b in begin_rows:
                b = jnp.broadcast_to(b[:, 0:1], slot.shape)
                found = jnp.where(slot >= b, jnp.maximum(found, b), found)
            return found

        slot = lax.broadcasted_iota(I32, dist.shape, 0) - MSLOT
        dist[...] = slot - doc_begin(slot)
        slot = lax.broadcasted_iota(I32, near.shape, 0)
        until = jnp.full(slot.shape, BIG, I32)
        for b in begin_rows:
            b = jnp.broadcast_to(b[:, 0:1], slot.shape)
            until = jnp.where(slot < b, jnp.minimum(until, b), until)
        near[...] = jnp.where(slot < fill, jnp.minimum(until, end) - 1 - slot, -1)
        for b, count in ((0, 128), (1, 128), (2, 16)):
            shape = (count, 256)
            a = lax.broadcasted_iota(I32, shape, 0)
            lane = lax.broadcasted_iota(I32, shape, 1)
            p, source = 128 * b + a, 128 * (b - 1) + lane
            j = p - source
            keep = (j >= 0) & (j < FILT) & (source >= doc_begin(p))
            maskf[128 * b:128 * b + count, :] = keep.astype(F32).astype(BF16)
            later = 128 * b + lane
            j = later - p
            begin = jnp.where(later < end, doc_begin(later), BIG)
            keep = (j >= 0) & (j < FILT) & (p >= begin)
            maskb[128 * b:128 * b + count, :] = keep.astype(F32).astype(BF16)
            if b < 2:
                p = 128 * b + 127 - a
                j = later - p
                maskp[128 * b:128 * b + count, :] = ((j >= 0) & (j < FILT) & (p >= begin)).astype(F32)
        r = lax.broadcasted_iota(I32, shift.shape, 0) + 192
        shift[...] = (r - fill == lax.broadcasted_iota(I32, shift.shape, 1)).astype(F32).astype(BF16)
        m[MSLOT + OUT:, :] = jnp.zeros((m.shape[0] - MSLOT - OUT, LANES), BF16)
        gx[WIN:, :] = jnp.zeros((gx.shape[0] - WIN, LANES), BF16)
        taps[...] = taps_ref[...].astype(F32)

    for part, (begin, _) in enumerate(PARTS):

        @pl.when(step == begin)
        def _():
            for c in head_copies(peers, part, qw_ref, kw_ref, vw_ref, gw_ref, hp, hsend, hrecv):
                c.wait()
            for c in tail_copies(peers, part, tails, hn, hsend, hrecv):
                c.wait()

    def own_or_next(ref, moved, begin, count):
        slot = lax.broadcasted_iota(I32, (count, LANES), 0) + begin
        return jnp.where(slot < fill, ref[begin:begin + count, :].astype(F32), moved)

    lanes = pl.ds(pl.multiple_of(step * LANES, LANES), LANES)
    kx[0:OFF, :] = hn[0:HALO, lanes].astype(F32)
    vx[0:OFF, :] = hn[HALO:2 * HALO, lanes].astype(F32)
    qx[0:QOFF, :] = hn[2 * HALO:2 * HALO + NEAR, lanes].astype(F32)
    moved_q = jnp.dot(shift[...], hp[0:HALO, lanes], preferred_element_type=F32)
    moved_g = jnp.dot(shift[...], hp[HALO:2 * HALO, lanes], preferred_element_type=F32)
    moved_k = jnp.dot(shift[0:80, 0:NEAR], hp[2 * HALO:2 * HALO + NEAR, lanes], preferred_element_type=F32)
    moved_v = jnp.dot(shift[0:80, 0:NEAR], hp[2 * HALO + NEAR:2 * HALO + 2 * NEAR, lanes], preferred_element_type=F32)
    for ref, out, off, moved in ((q_ref, qx, QOFF, moved_q), (g_ref, gw, 0, moved_g), (k_ref, kx, OFF, moved_k), (v_ref, vx, OFF, moved_v)):
        out[off:off + 192, :] = ref[0:192, :].astype(F32)
        out[off + 192:off + 256, :] = own_or_next(ref, moved[0:64], 192, 64)
        out[off + 256:off + 192 + moved.shape[0], :] = moved[64:]

    feat = [ft_ref[w, :, lanes].astype(F32) for w in range(3)]
    block = 16

    def featurize(window, at, far, w):
        acc = feat[w][0:1, :] * window[at:at + block, :]
        for j in range(1, SHORT):
            acc = acc + jnp.where(far >= j, feat[w][j:j + 1, :] * window[at - j:at - j + block, :], 0.0)
        return acc

    for s in range(-MSLOT, OUT, block):
        far = dist[s + MSLOT:s + MSLOT + block, :]
        key_rows = featurize(kx, OFF + s, far, 1)
        value_rows = featurize(vx, OFF + s, far, 2)
        m[MSLOT + s:MSLOT + s + block, :] = (key_rows * value_rows).astype(BF16)
        if s >= 0:
            keys[s:s + block, :] = key_rows
            values[s:s + block, :] = value_rows
    for s in range(0, WIN, block):
        far = dist[s + MSLOT:s + MSLOT + block, :]
        query_rows = featurize(qx, QOFF + s, far, 0)
        gx[s:s + block, :] = (query_rows * gw[s:s + block, :]).astype(BF16)
        if s < rows:
            query[s:s + block, :] = query_rows

    flip = (lax.broadcasted_iota(I32, (128, 128), 0) + lax.broadcasted_iota(I32, (128, 128), 1)) == 127
    for at in range(0, rows, 128):
        inside = lax.broadcasted_iota(I32, (128, 128), 1) + at < fill
        pick = jnp.where(flip & inside, 1.0, 0.0).astype(BF16)
        mown[at:at + 128, :] = jnp.dot(pick, m[MSLOT + at:MSLOT + at + 128, :], preferred_element_type=F32).astype(BF16)

    group_of = lax.broadcasted_iota(I32, (128, LANES), 1) // GROUP
    my_taps = taps[pl.ds(pl.multiple_of(step * 8, 8), 8), :]
    reverse = (lax.broadcasted_iota(I32, (FILT, FILT), 0) + lax.broadcasted_iota(I32, (FILT, FILT), 1)) % FILT == 0
    turned = jnp.dot(my_taps.astype(BF16), reverse.astype(F32).astype(BF16), preferred_element_type=F32)

    def circulant(row):
        return pltpu.roll(jnp.broadcast_to(row, (FILT, FILT)), 0, 1, stride=1, stride_axis=0)

    blocks = ((0, 128), (1, 128), (2, 16))
    skip = skip_ref[...]

    acc = [jnp.zeros((count, LANES), F32) for _, count in blocks]
    for g in range(8):
        circ = circulant(turned[g:g + 1, :]).astype(BF16)
        for b, count in blocks:
            both = jnp.concatenate([circ[:count], circ[:count]], axis=1) * maskf[128 * b:128 * b + count, :]
            res = jnp.dot(both, m[128 * b:128 * b + 256, :], preferred_element_type=F32)
            acc[b] = jnp.where(group_of[:count] == g, res, acc[b])
    for b, count in blocks:
        at = 128 * b
        gated = acc[b] + skip * m[MSLOT + at:MSLOT + at + count, :].astype(F32)
        qb[step, at:at + count, :] = (gw[at:at + count, :] * gated).astype(BF16).astype(F32)
        if b < 2:
            inside = lax.broadcasted_iota(I32, (count, LANES), 0) + at < fill
            ho_ref[at:at + count, :] = jnp.where(inside, query[at:at + count, :] * gated, 0.0).astype(BF16)

    acc = [jnp.zeros((count, LANES), F32) for _, count in blocks]
    mix_rows = []
    for g in range(8):
        circ = circulant(my_taps[g:g + 1, :]).astype(BF16)
        fold = jnp.zeros((128, FILT), F32)
        for b, count in blocks:
            both = jnp.concatenate([circ[:count], circ[:count]], axis=1) * maskb[128 * b:128 * b + count, :]
            window = gx[128 * b:128 * b + 256, :]
            res = jnp.dot(both, window, preferred_element_type=F32)
            acc[b] = jnp.where(group_of[:count] == g, res, acc[b])
            if b < 2:
                mine = jnp.where(group_of == g, mown[128 * b:128 * b + 128, :], jnp.zeros((), BF16))
                prod = lax.dot_general(mine, window, (((1,), (1,)), ((), ())), preferred_element_type=F32)
                prod = prod * maskp[128 * b:128 * b + 128, :]
                fold = fold + prod[:, :128] + prod[:, 128:]
        turned_back = pltpu.roll(fold, 1, 1, stride=1, stride_axis=0)
        mix_rows.append(jnp.sum(turned_back, axis=0, keepdims=True))
    for b, count in blocks:
        at = 128 * b
        back = acc[b] + skip * gx[at:at + count, :].astype(F32)
        kb[step, at:at + count, :] = (back * values[at:at + count, :]).astype(BF16).astype(F32)
        vb[step, at:at + count, :] = (back * keys[at:at + count, :]).astype(BF16).astype(F32)

    slot = lax.broadcasted_iota(I32, (rows, LANES), 0)
    both = m[MSLOT:MSLOT + rows, :].astype(F32) * gx[0:rows, :].astype(F32)
    skip_row = jnp.sum(jnp.where(slot < fill, both, 0.0), axis=0, keepdims=True)
    feat_rows = []
    for w, (back, window, off) in enumerate(((qb, qx, QOFF), (kb, kx, OFF), (vb, vx, OFF))):
        sums = [jnp.zeros((block, LANES), F32) for _ in range(SHORT)]
        for s in range(0, rows, block):
            reach = near[s:s + block, :]
            source = window[off + s:off + s + block, :]
            for j in range(SHORT):
                later = jnp.where(reach >= j, back[step, s + j:s + j + block, :], 0.0)
                sums[j] = sums[j] + source * later
        feat_rows += [jnp.sum(x, axis=0, keepdims=True) for x in sums]
    packed = jnp.concatenate(mix_rows + [skip_row] + feat_rows + [jnp.zeros((2, LANES), F32)], axis=0)
    for i in range(2):
        piece = 2 * step + i
        raw[piece] = packed[16 * i:16 * i + 16]
        e, device = peers.owner(piece)

        @pl.when(e != 0)
        def _():
            piece_copy(raw, got, s1, r1, piece, e, device).start()

    @pl.when(step == pl.num_programs(0) - 1)
    def _():
        outs = []
        for w, (back, ref, hbm) in enumerate(((qb, qo, qg_ref), (kb, ko, kg_ref), (vb, vo, vg_ref))):

            def chunk(i, carry):
                cols = pl.ds(pl.multiple_of(i * LANES, LANES), LANES)
                weight = ft_ref[w, :, cols].astype(F32)
                for s in range(0, rows, block):
                    reach = near[s:s + block, :]
                    acc = jnp.zeros((block, LANES), F32)
                    for j in range(SHORT):
                        later = jnp.where(reach >= j, back[i, s + j:s + j + block, :], 0.0)
                        acc = acc + weight[j:j + 1, :] * later
                    ref[s:s + block, cols] = acc.astype(BF16)
                return carry

            lax.fori_loop(0, pl.num_programs(0), chunk, 0)
            outs.append(pltpu.make_async_copy(ref, hbm, load_sem.at[w]))
            outs[w].start()
        sum_shards(peers, params, raw, got, parts, full, squares, s1, r1, s2, r2, s3, r3, s4, r4, pk_ref)
        for c in outs:
            c.wait()


def mix_call(nz, ntp, params, fill, docs, q, k, v, g, ft, taps, skip):
    rows, ch = q.shape
    steps = ch // LANES
    col = lambda count: pl.BlockSpec((count, LANES), lambda i: (0, i))
    smem = pl.BlockSpec(memory_space=pltpu.SMEM)
    hbm = pl.BlockSpec(memory_space=pl.ANY)
    dma = pltpu.SemaphoreType.DMA
    piece = (16, LANES)
    return pl.pallas_call(
        lambda *refs: mix_kernel(nz, ntp, params, *refs),
        grid=(steps,),
        out_shape=tuple(jax.ShapeDtypeStruct((rows, ch), BF16) for _ in range(4))
        + (jax.ShapeDtypeStruct((NEAREST, *piece), F32),),
        in_specs=[smem, smem, hbm, hbm, hbm, hbm, col(rows), col(rows), col(rows), col(rows),
                  pl.BlockSpec(ft.shape, lambda i: (0, 0, 0)), pl.BlockSpec(taps.shape, lambda i: (0, 0)), col(1)],
        out_specs=(col(rows), hbm, hbm, hbm, pl.BlockSpec((NEAREST, *piece), lambda i: (0, 0, 0))),
        scratch_shapes=[
            pltpu.VMEM((QOFF + WIN, LANES), F32),
            pltpu.VMEM((OFF + OUT, LANES), F32),
            pltpu.VMEM((OFF + OUT, LANES), F32),
            pltpu.VMEM((WIN, LANES), F32),
            pltpu.VMEM((rows, LANES), F32),
            pltpu.VMEM((OUT, LANES), F32),
            pltpu.VMEM((OUT, LANES), F32),
            pltpu.VMEM((steps, OUT, LANES), F32),
            pltpu.VMEM((steps, OUT, LANES), F32),
            pltpu.VMEM((steps, OUT, LANES), F32),
            pltpu.VMEM((512, LANES), BF16),
            pltpu.VMEM((512, LANES), BF16),
            pltpu.VMEM((rows, LANES), BF16),
            pltpu.VMEM((MSLOT + WIN, LANES), I32),
            pltpu.VMEM((rows, LANES), I32),
            pltpu.VMEM((OUT, 256), BF16),
            pltpu.VMEM((OUT, 256), BF16),
            pltpu.VMEM((rows, 256), F32),
            pltpu.VMEM((WIN - 192, HALO), BF16),
            pltpu.VMEM(taps.shape, F32),
            pltpu.VMEM((rows, ch), BF16),
            pltpu.VMEM((rows, ch), BF16),
            pltpu.VMEM((rows, ch), BF16),
            pltpu.VMEM((1, LANES), I32),
            pltpu.VMEM((2 * HALO + NEAR, ch), BF16),
            pltpu.VMEM((2 * HALO + 2 * NEAR, ch), BF16),
            pltpu.VMEM((3, rows, ch), BF16),
            pltpu.VMEM((2 * HALO + NEAR, ch), BF16),
            pltpu.VMEM((nz, NY, 1, LANES), I32),
            pltpu.VMEM((NEAREST, *piece), F32),
            pltpu.VMEM((NEAREST, *piece), F32),
            pltpu.VMEM((nz // NZB, *piece), F32),
            pltpu.VMEM((NEAREST, *piece), F32),
            pltpu.VMEM((ntp // 2, 2, 1, LANES), F32),
            dma((3,)), dma((NY,)), dma((NY,)), dma((nz,)), dma((nz,)), dma((len(PARTS), 7)), dma((len(PARTS), 7)),
            dma((NEAREST,)), dma((NEAREST,)), dma((nz // NZB,)), dma((nz // NZB,)), dma((NEAREST,)), dma((NEAREST,)),
            dma((ntp,)), dma((ntp,)),
        ],
        compiler_params=pltpu.CompilerParams(collective_id=0, has_side_effects=True, vmem_limit_bytes=60 << 20),
        name="mix",
    )(fill, docs, q, k, v, g, q, k, v, g, ft, taps, skip)


def place_kernel(*refs):
    big, pk_ref, outs = refs[:4], refs[4], refs[5:9]
    mix_ref, skip_ref, feat_ref, held, load, store = refs[9:]
    half = held.shape[1] // 2
    moves = [(i, j, pl.ds(half * j, half)) for j in range(2) for i in range(4)]
    loads = [pltpu.make_async_copy(big[i].at[part], held.at[i, part], load.at[i, j]) for i, j, part in moves]
    stores = [pltpu.make_async_copy(held.at[i, part], outs[i].at[part], store.at[i, j]) for i, j, part in moves]
    for c in loads:
        c.start()
    for c, d in zip(loads, stores):
        c.wait()
        d.start()
    for k in range(pk_ref.shape[0] // 2):
        lanes = slice(LANES * k, LANES * k + LANES)
        mix_ref[8 * k:8 * k + 8, :] = pk_ref[2 * k, 0:8]
        skip_ref[:, lanes] = pk_ref[2 * k, 8:9]
        for w in range(3):
            for j in range(SHORT):
                r = 9 + SHORT * w + j
                feat_ref[w, j:j + 1, lanes] = pk_ref[2 * k + r // 16, r % 16:r % 16 + 1]
    for d in stores:
        d.wait()


def place_call(big, pk, groups):
    rows, ch = big[0].shape
    vmem, hbm = pl.BlockSpec(memory_space=pltpu.VMEM), pl.BlockSpec(memory_space=pl.ANY)
    return pl.pallas_call(
        place_kernel,
        out_shape=tuple(jax.ShapeDtypeStruct((rows, ch), BF16) for _ in range(4)) + (
            jax.ShapeDtypeStruct((groups, FILT), F32),
            jax.ShapeDtypeStruct((1, ch), F32),
            jax.ShapeDtypeStruct((3, SHORT, ch), F32),
        ),
        in_specs=[hbm] * 4 + [vmem],
        out_specs=(hbm,) * 4 + (vmem,) * 3,
        scratch_shapes=[pltpu.VMEM((4, rows, ch), BF16), pltpu.SemaphoreType.DMA((4, 2)), pltpu.SemaphoreType.DMA((4, 2))],
        compiler_params=pltpu.CompilerParams(vmem_limit_bytes=60 << 20),
        name="place",
    )(*big, pk)


def solution(mesh):
    n, ntp = mesh.shape["ctx"], mesh.shape["tp"]
    nz = n // NY

    def shards(q, k, v, g, fill, docs, ft, taps, skip):
        groups, ch = taps.shape[0], q.shape[1]
        params = (groups * FILT + ch * (1 + 3 * SHORT)) * ntp
        *big, pk = mix_call(nz, ntp, params, fill, docs, q, k, v, g, ft, taps, skip.reshape(1, ch))
        *big, mix_grad, skip_grad, feat_grad = place_call(big, pk, groups)
        return *big, mix_grad, skip_grad.reshape(ch), feat_grad

    rows, whole = P("ctx", "tp"), P(None, None, "tp")
    return jax.shard_map(
        shards, mesh=mesh,
        in_specs=(rows, rows, rows, rows, P("ctx"), P(), whole, P("tp", None), P("tp")),
        out_specs=(rows, rows, rows, rows, P("tp", None), P("tp"), whole),
        check_vma=False)
```

```python
import jax
import jax.numpy as jnp
from jax import lax
from jax.experimental import pallas as pl
from jax.experimental.pallas import tpu as pltpu
from jax.sharding import PartitionSpec as P

F32 = jnp.float32
BF16 = jnp.bfloat16
I32 = jnp.int32
MESH = pl.DeviceIdType.MESH

NY = 4
HALO = 144
NEAR = 16
LANES = 128
SHORT = 7
FILT = 128
GROUP = 16
BIG = 1 << 28

OFF = HALO
QOFF = NEAR
OUT = 272
WIN = 400
MSLOT = 128

NEAREST = 16
NZB = 4
PARTS = ((0, 1), (1, 3), (3, 8))
TAILS = (HALO, HALO, NEAR)


def mesh_copy(src, dst, ssem, rsem, device):
    c = pltpu.make_async_remote_copy(src_ref=src, dst_ref=dst, send_sem=ssem, recv_sem=rsem,
                                     device_id=device, device_id_type=MESH)
    c.start()
    return c


def piece_copy(raw, got, s1, r1, piece, e, device):
    return pltpu.make_async_remote_copy(src_ref=raw.at[piece], dst_ref=got.at[e], send_sem=s1.at[e], recv_sem=r1.at[e],
                                        device_id=device, device_id_type=MESH)


class Peers:
    def __init__(self, nz, ntp):
        self.nz, self.ntp = nz, ntp
        self.me = lax.axis_index("ctx")
        self.tp = lax.axis_index("tp")
        self.z, self.y = self.me // NY, self.me % NY
        self.za, self.zb = self.z // NZB, self.z % NZB
        self.nza = nz // NZB

    def along_y(self, d):
        return {"ctx": self.z * NY + lax.rem(self.y + d, NY)}

    def along_z(self, d):
        return {"ctx": lax.rem(self.z + d, self.nz) * NY + self.y}

    def step(self, d):
        return {"ctx": lax.rem(self.me + d + self.nz * NY, self.nz * NY)}

    def near(self, e):
        y, zb = lax.rem(self.y + e // NZB, NY), lax.rem(self.zb + e % NZB, NZB)
        return y * NZB + zb, {"ctx": (self.za * NZB + zb) * NY + y}

    def far(self, d):
        return {"ctx": (lax.rem(self.za + d, self.nza) * NZB + self.zb) * NY + self.y}

    def owner(self, piece):
        y, zb = piece // NZB, piece % NZB
        e = lax.rem(y - self.y + NY, NY) * NZB + lax.rem(zb - self.zb + NZB, NZB)
        return e, {"ctx": (self.za * NZB + zb) * NY + y}

    def other_core(self):
        return {"tp": self.tp + 1 - 2 * (self.tp % 2)}

    def along_x(self, d):
        return {"tp": lax.rem(self.tp + 2 * d, self.ntp)}


def exchange(at, fill, q_ref, k_ref, v_ref, g_ref, first, hn, hp, vbuf, tails, counts,
             load_sem, ysend, yrecv, zsend, zrecv, hsend, hrecv):
    nz, rows = at.nz, q_ref.shape[0]
    loads = []
    for i, ref in enumerate((q_ref, k_ref, v_ref, g_ref)):
        c = pltpu.make_async_copy(ref, vbuf.at[i], load_sem.at[i])
        c.start()
        loads.append(c)

    barrier = pltpu.get_barrier_semaphore()
    partners = [at.along_y(d) for d in range(1, NY)] + [at.along_z(d) for d in range(1, nz)] + [at.step(1), at.step(-1)]
    partners += [at.near(e)[1] for e in range(1, NEAREST)] + [at.other_core()] + [at.along_x(d) for d in range(1, at.ntp // 2)]
    for device in partners:
        pl.semaphore_signal(barrier, inc=1, device_id=device, device_id_type=MESH)
    counts[at.z, at.y] = jnp.full((1, LANES), fill, I32)
    pl.semaphore_wait(barrier, len(partners))

    own = counts.at[at.z, at.y]
    ycopies = [mesh_copy(own, own, ysend.at[d], yrecv.at[d], at.along_y(d)) for d in range(1, NY)]
    for c in head_copies(at, 0, q_ref, k_ref, v_ref, g_ref, hp, hsend, hrecv):
        c.start()
    row = 0
    for i, count in zip((1, 2, 0), TAILS):
        loads[i].wait()
        slot = lax.broadcasted_iota(I32, (count, rows), 0) + (fill - count)
        pick = (slot == lax.broadcasted_iota(I32, (count, rows), 1)).astype(F32).astype(BF16)
        tails[row:row + count, :] = jnp.dot(pick, vbuf[i], preferred_element_type=F32).astype(BF16)
        row += count
    for c in tail_copies(at, 0, tails, hn, hsend, hrecv):
        c.start()
    for c in ycopies:
        c.wait()
    own = counts.at[at.z]
    zcopies = [mesh_copy(own, own, zsend.at[d], zrecv.at[d], at.along_z(d)) for d in range(1, nz)]
    for part in range(1, len(PARTS)):
        for c in head_copies(at, part, q_ref, k_ref, v_ref, g_ref, hp, hsend, hrecv):
            c.start()
        for c in tail_copies(at, part, tails, hn, hsend, hrecv):
            c.start()
    for c in zcopies:
        c.wait()
    loads[3].wait()
    shard = lax.broadcasted_iota(I32, counts.shape, 0) * NY + lax.broadcasted_iota(I32, counts.shape, 1)
    first[...] = jnp.sum(jnp.where(shard < at.me, counts[...], 0), axis=(0, 1))


def head_copies(at, part, q_ref, k_ref, v_ref, g_ref, hp, hsend, hrecv):
    copies, row = [], 0
    cols = pl.ds(PARTS[part][0] * LANES, (PARTS[part][1] - PARTS[part][0]) * LANES)
    for i, (ref, count) in enumerate(((q_ref, HALO), (g_ref, HALO), (k_ref, NEAR), (v_ref, NEAR))):
        copies.append(pltpu.make_async_remote_copy(
            src_ref=ref.at[pl.ds(0, count), cols], dst_ref=hp.at[pl.ds(row, count), cols],
            send_sem=hsend.at[part, i], recv_sem=hrecv.at[part, i], device_id=at.step(-1), device_id_type=MESH))
        row += count
    return copies


def tail_copies(at, part, tails, hn, hsend, hrecv):
    copies, row = [], 0
    cols = pl.ds(PARTS[part][0] * LANES, (PARTS[part][1] - PARTS[part][0]) * LANES)
    for i, count in enumerate(TAILS):
        rows = pl.ds(row, count)
        copies.append(pltpu.make_async_remote_copy(
            src_ref=tails.at[rows, cols], dst_ref=hn.at[rows, cols],
            send_sem=hsend.at[part, 4 + i], recv_sem=hrecv.at[part, 4 + i], device_id=at.step(1), device_id_type=MESH))
        row += count
    return copies


def sum_shards(at, params, meanwhile, raw, got, parts, full, squares, s1, r1, s2, r2, s3, r3, s4, r4, out_ref):
    mine = at.y * NZB + at.zb
    for e in range(1, NEAREST):
        piece, device = at.near(e)
        piece_copy(raw, got, s1, r1, piece, e, device).wait()
    acc = raw[mine]
    for e in range(1, NEAREST):
        acc = acc + got[e]
    parts[at.za] = acc
    own = parts.at[at.za]
    copies = [mesh_copy(own, own, s2.at[d], r2.at[d], at.far(d)) for d in range(1, at.nza)]
    meanwhile()
    for c in copies:
        c.wait()
    acc = parts[0]
    for d in range(1, at.nza):
        acc = acc + parts[d]
    full[mine] = acc
    own = full.at[mine]
    copies = [mesh_copy(own, own, s3.at[e], r3.at[e], at.near(e)[1]) for e in range(1, NEAREST)]
    for c in copies:
        c.wait()
    square = jnp.zeros(full.shape[1:], F32)
    for i in range(NEAREST):
        square = square + full[i] * full[i]
    square = jnp.sum(jnp.sum(square, axis=0, keepdims=True), axis=1, keepdims=True)
    chip, core = at.tp // 2, at.tp % 2
    squares[chip, core] = jnp.broadcast_to(square, (1, LANES))
    own = squares.at[chip, core]
    mesh_copy(own, own, s4.at[0], r4.at[0], at.other_core()).wait()
    own = squares.at[chip]
    copies = [mesh_copy(own, own, s4.at[d], r4.at[d], at.along_x(d)) for d in range(1, at.ntp // 2)]
    for c in copies:
        c.wait()
    factor = lax.rsqrt(jnp.sum(squares[...], axis=(0, 1)) / params + 1e-06)
    for i in range(NEAREST):
        out_ref[i] = full[i] * factor


def mix_kernel(nz, ntp, params, fill_ref, docs_ref, q_ref, k_ref, v_ref, g_ref, ft_ref, taps_ref, skip_ref,
               ho_ref, qg_ref, kg_ref, vg_ref, pk_ref,
               qx, kx, vx, gw, query, keys, values, qb, kb, vb, m, gx, mown, dist, near, maskf, maskb, maskp, shift, taps, vout,
               first_row, hn, hp, vbuf, tails, counts, raw, got, parts, full, squares,
               load_sem, ysend, yrecv, zsend, zrecv, hsend, hrecv, s1, r1, s2, r2, s3, r3, s4, r4):
    step = pl.program_id(0)
    rows = q_ref.shape[0]
    fill = fill_ref[0]
    peers = Peers(nz, ntp)
    last = peers.me == nz * NY - 1

    @pl.when(step == 0)
    def _():
        exchange(peers, fill, q_ref, k_ref, v_ref, g_ref, first_row, hn, hp, vbuf, tails, counts,
                 load_sem, ysend, yrecv, zsend, zrecv, hsend, hrecv)
        begin_rows = [docs_ref[i] - first_row[...] for i in range(docs_ref.shape[0])]
        end = jnp.where(last, fill, BIG)

        def doc_begin(slot):
            found = jnp.full(slot.shape, -BIG, I32)
            for b in begin_rows:
                b = jnp.broadcast_to(b[:, 0:1], slot.shape)
                found = jnp.where(slot >= b, jnp.maximum(found, b), found)
            return found

        slot = lax.broadcasted_iota(I32, dist.shape, 0) - MSLOT
        dist[...] = slot - doc_begin(slot)
        slot = lax.broadcasted_iota(I32, near.shape, 0)
        until = jnp.full(slot.shape, BIG, I32)
        for b in begin_rows:
            b = jnp.broadcast_to(b[:, 0:1], slot.shape)
            until = jnp.where(slot < b, jnp.minimum(until, b), until)
        near[...] = jnp.where(slot < fill, jnp.minimum(until, end) - 1 - slot, -1)
        for b, count in ((0, 128), (1, 128), (2, 16)):
            shape = (count, 256)
            a = lax.broadcasted_iota(I32, shape, 0)
            lane = lax.broadcasted_iota(I32, shape, 1)
            p, source = 128 * b + a, 128 * (b - 1) + lane
            j = p - source
            keep = (j >= 0) & (j < FILT) & (source >= doc_begin(p))
            maskf[128 * b:128 * b + count, :] = keep.astype(F32).astype(BF16)
            later = 128 * b + lane
            j = later - p
            begin = jnp.where(later < end, doc_begin(later), BIG)
            keep = (j >= 0) & (j < FILT) & (p >= begin)
            maskb[128 * b:128 * b + count, :] = keep.astype(F32).astype(BF16)
            if b < 2:
                p = 128 * b + 127 - a
                j = later - p
                maskp[128 * b:128 * b + count, :] = ((j >= 0) & (j < FILT) & (p >= begin)).astype(F32)
        r = lax.broadcasted_iota(I32, shift.shape, 0) + 192
        shift[...] = (r - fill == lax.broadcasted_iota(I32, shift.shape, 1)).astype(F32).astype(BF16)
        m[MSLOT + OUT:, :] = jnp.zeros((m.shape[0] - MSLOT - OUT, LANES), BF16)
        gx[WIN:, :] = jnp.zeros((gx.shape[0] - WIN, LANES), BF16)
        taps[...] = taps_ref[...].astype(F32)

    for part, (begin, _) in enumerate(PARTS):

        @pl.when(step == begin)
        def _():
            for c in head_copies(peers, part, q_ref, k_ref, v_ref, g_ref, hp, hsend, hrecv):
                c.wait()
            for c in tail_copies(peers, part, tails, hn, hsend, hrecv):
                c.wait()

    def own_or_next(i, moved, begin, count):
        slot = lax.broadcasted_iota(I32, (count, LANES), 0) + begin
        return jnp.where(slot < fill, vbuf[i, begin:begin + count, lanes].astype(F32), moved)

    lanes = pl.ds(pl.multiple_of(step * LANES, LANES), LANES)
    kx[0:OFF, :] = hn[0:HALO, lanes].astype(F32)
    vx[0:OFF, :] = hn[HALO:2 * HALO, lanes].astype(F32)
    qx[0:QOFF, :] = hn[2 * HALO:2 * HALO + NEAR, lanes].astype(F32)
    moved_q = jnp.dot(shift[...], hp[0:HALO, lanes], preferred_element_type=F32)
    moved_g = jnp.dot(shift[...], hp[HALO:2 * HALO, lanes], preferred_element_type=F32)
    moved_k = jnp.dot(shift[0:80, 0:NEAR], hp[2 * HALO:2 * HALO + NEAR, lanes], preferred_element_type=F32)
    moved_v = jnp.dot(shift[0:80, 0:NEAR], hp[2 * HALO + NEAR:2 * HALO + 2 * NEAR, lanes], preferred_element_type=F32)
    windows = ((qx, QOFF, moved_q), (kx, OFF, moved_k), (vx, OFF, moved_v), (gw, 0, moved_g))
    for i, (out, off, moved) in enumerate(windows):
        out[off:off + 192, :] = vbuf[i, 0:192, lanes].astype(F32)
        out[off + 192:off + 256, :] = own_or_next(i, moved[0:64], 192, 64)
        out[off + 256:off + 192 + moved.shape[0], :] = moved[64:]

    feat = [ft_ref[w, :, lanes].astype(F32) for w in range(3)]
    block = 16

    def featurize(window, at, far, w):
        acc = feat[w][0:1, :] * window[at:at + block, :]
        for j in range(1, SHORT):
            acc = acc + jnp.where(far >= j, feat[w][j:j + 1, :] * window[at - j:at - j + block, :], 0.0)
        return acc

    for s in range(-MSLOT, OUT, block):
        far = dist[s + MSLOT:s + MSLOT + block, :]
        key_rows = featurize(kx, OFF + s, far, 1)
        value_rows = featurize(vx, OFF + s, far, 2)
        m[MSLOT + s:MSLOT + s + block, :] = (key_rows * value_rows).astype(BF16)
        if s >= 0:
            keys[s:s + block, :] = key_rows
            values[s:s + block, :] = value_rows
    for s in range(0, WIN, block):
        far = dist[s + MSLOT:s + MSLOT + block, :]
        query_rows = featurize(qx, QOFF + s, far, 0)
        gx[s:s + block, :] = (query_rows * gw[s:s + block, :]).astype(BF16)
        if s < rows:
            query[s:s + block, :] = query_rows

    flip = (lax.broadcasted_iota(I32, (128, 128), 0) + lax.broadcasted_iota(I32, (128, 128), 1)) == 127
    for at in range(0, rows, 128):
        inside = lax.broadcasted_iota(I32, (128, 128), 1) + at < fill
        pick = jnp.where(flip & inside, 1.0, 0.0).astype(BF16)
        mown[at:at + 128, :] = jnp.dot(pick, m[MSLOT + at:MSLOT + at + 128, :], preferred_element_type=F32).astype(BF16)

    group_of = lax.broadcasted_iota(I32, (128, LANES), 1) // GROUP
    my_taps = taps[pl.ds(pl.multiple_of(step * 8, 8), 8), :]
    reverse = (lax.broadcasted_iota(I32, (FILT, FILT), 0) + lax.broadcasted_iota(I32, (FILT, FILT), 1)) % FILT == 0
    turned = jnp.dot(my_taps.astype(BF16), reverse.astype(F32).astype(BF16), preferred_element_type=F32)

    def circulant(row):
        return pltpu.roll(jnp.broadcast_to(row, (FILT, FILT)), 0, 1, stride=1, stride_axis=0)

    blocks = ((0, 128), (1, 128), (2, 16))
    skip = skip_ref[:, lanes]

    acc = [jnp.zeros((count, LANES), F32) for _, count in blocks]
    for g in range(8):
        circ = circulant(turned[g:g + 1, :]).astype(BF16)
        for b, count in blocks:
            both = jnp.concatenate([circ[:count], circ[:count]], axis=1) * maskf[128 * b:128 * b + count, :]
            res = jnp.dot(both, m[128 * b:128 * b + 256, :], preferred_element_type=F32)
            acc[b] = jnp.where(group_of[:count] == g, res, acc[b])
    for b, count in blocks:
        at = 128 * b
        gated = acc[b] + skip * m[MSLOT + at:MSLOT + at + count, :].astype(F32)
        qb[step, at:at + count, :] = (gw[at:at + count, :] * gated).astype(BF16).astype(F32)
        if b < 2:
            inside = lax.broadcasted_iota(I32, (count, LANES), 0) + at < fill
            vout[0, at:at + count, lanes] = jnp.where(inside, query[at:at + count, :] * gated, 0.0).astype(BF16)

    acc = [jnp.zeros((count, LANES), F32) for _, count in blocks]
    mix_rows = []
    for g in range(8):
        circ = circulant(my_taps[g:g + 1, :]).astype(BF16)
        fold = jnp.zeros((128, FILT), F32)
        for b, count in blocks:
            both = jnp.concatenate([circ[:count], circ[:count]], axis=1) * maskb[128 * b:128 * b + count, :]
            window = gx[128 * b:128 * b + 256, :]
            res = jnp.dot(both, window, preferred_element_type=F32)
            acc[b] = jnp.where(group_of[:count] == g, res, acc[b])
            if b < 2:
                mine = jnp.where(group_of == g, mown[128 * b:128 * b + 128, :], jnp.zeros((), BF16))
                prod = lax.dot_general(mine, window, (((1,), (1,)), ((), ())), preferred_element_type=F32)
                prod = prod * maskp[128 * b:128 * b + 128, :]
                fold = fold + prod[:, :128] + prod[:, 128:]
        turned_back = pltpu.roll(fold, 1, 1, stride=1, stride_axis=0)
        mix_rows.append(jnp.sum(turned_back, axis=0, keepdims=True))
    for b, count in blocks:
        at = 128 * b
        back = acc[b] + skip * gx[at:at + count, :].astype(F32)
        kb[step, at:at + count, :] = (back * values[at:at + count, :]).astype(BF16).astype(F32)
        vb[step, at:at + count, :] = (back * keys[at:at + count, :]).astype(BF16).astype(F32)

    slot = lax.broadcasted_iota(I32, (rows, LANES), 0)
    both = m[MSLOT:MSLOT + rows, :].astype(F32) * gx[0:rows, :].astype(F32)
    skip_row = jnp.sum(jnp.where(slot < fill, both, 0.0), axis=0, keepdims=True)
    feat_rows = []
    for w, (back, window, off) in enumerate(((qb, qx, QOFF), (kb, kx, OFF), (vb, vx, OFF))):
        sums = [jnp.zeros((block, LANES), F32) for _ in range(SHORT)]
        for s in range(0, rows, block):
            reach = near[s:s + block, :]
            source = window[off + s:off + s + block, :]
            for j in range(SHORT):
                later = jnp.where(reach >= j, back[step, s + j:s + j + block, :], 0.0)
                sums[j] = sums[j] + source * later
        feat_rows += [jnp.sum(x, axis=0, keepdims=True) for x in sums]
    packed = jnp.concatenate(mix_rows + [skip_row] + feat_rows + [jnp.zeros((2, LANES), F32)], axis=0)
    for i in range(2):
        piece = 2 * step + i
        raw[piece] = packed[16 * i:16 * i + 16]
        e, device = peers.owner(piece)

        @pl.when(e != 0)
        def _():
            piece_copy(raw, got, s1, r1, piece, e, device).start()

    @pl.when(step == pl.num_programs(0) - 1)
    def _():
        outs = [pltpu.make_async_copy(vout.at[i], ref, load_sem.at[i]) for i, ref in enumerate((ho_ref, qg_ref, kg_ref, vg_ref))]

        def meanwhile():
            outs[0].start()
            for w, back in enumerate((qb, kb, vb)):

                def chunk(i, carry):
                    cols = pl.ds(pl.multiple_of(i * LANES, LANES), LANES)
                    weight = ft_ref[w, :, cols].astype(F32)
                    for s in range(0, rows, block):
                        reach = near[s:s + block, :]
                        acc = jnp.zeros((block, LANES), F32)
                        for j in range(SHORT):
                            later = jnp.where(reach >= j, back[i, s + j:s + j + block, :], 0.0)
                            acc = acc + weight[j:j + 1, :] * later
                        vout[1 + w, s:s + block, cols] = acc.astype(BF16)
                    return carry

                lax.fori_loop(0, pl.num_programs(0), chunk, 0)
                outs[1 + w].start()

        sum_shards(peers, params, meanwhile, raw, got, parts, full, squares, s1, r1, s2, r2, s3, r3, s4, r4, pk_ref)
        for c in outs:
            c.wait()


def mix_call(nz, ntp, params, fill, docs, q, k, v, g, ft, taps, skip):
    rows, ch = q.shape
    steps = ch // LANES
    smem = pl.BlockSpec(memory_space=pltpu.SMEM)
    hbm = pl.BlockSpec(memory_space=pl.ANY)
    dma = pltpu.SemaphoreType.DMA
    piece = (16, LANES)
    return pl.pallas_call(
        lambda *refs: mix_kernel(nz, ntp, params, *refs),
        grid=(steps,),
        out_shape=tuple(jax.ShapeDtypeStruct((rows, ch), BF16) for _ in range(4))
        + (jax.ShapeDtypeStruct((NEAREST, *piece), F32),),
        in_specs=[smem, smem, hbm, hbm, hbm, hbm,
                  pl.BlockSpec(ft.shape, lambda i: (0, 0, 0)), pl.BlockSpec(taps.shape, lambda i: (0, 0)),
                  pl.BlockSpec(skip.shape, lambda i: (0, 0))],
        out_specs=(hbm, hbm, hbm, hbm, pl.BlockSpec((NEAREST, *piece), lambda i: (0, 0, 0))),
        scratch_shapes=[
            pltpu.VMEM((QOFF + WIN, LANES), F32),
            pltpu.VMEM((OFF + OUT, LANES), F32),
            pltpu.VMEM((OFF + OUT, LANES), F32),
            pltpu.VMEM((WIN, LANES), F32),
            pltpu.VMEM((rows, LANES), F32),
            pltpu.VMEM((OUT, LANES), F32),
            pltpu.VMEM((OUT, LANES), F32),
            pltpu.VMEM((steps, OUT, LANES), F32),
            pltpu.VMEM((steps, OUT, LANES), F32),
            pltpu.VMEM((steps, OUT, LANES), F32),
            pltpu.VMEM((512, LANES), BF16),
            pltpu.VMEM((512, LANES), BF16),
            pltpu.VMEM((rows, LANES), BF16),
            pltpu.VMEM((MSLOT + WIN, LANES), I32),
            pltpu.VMEM((rows, LANES), I32),
            pltpu.VMEM((OUT, 256), BF16),
            pltpu.VMEM((OUT, 256), BF16),
            pltpu.VMEM((rows, 256), F32),
            pltpu.VMEM((WIN - 192, HALO), BF16),
            pltpu.VMEM(taps.shape, F32),
            pltpu.VMEM((4, rows, ch), BF16),
            pltpu.VMEM((1, LANES), I32),
            pltpu.VMEM((2 * HALO + NEAR, ch), BF16),
            pltpu.VMEM((2 * HALO + 2 * NEAR, ch), BF16),
            pltpu.VMEM((4, rows, ch), BF16),
            pltpu.VMEM((2 * HALO + NEAR, ch), BF16),
            pltpu.VMEM((nz, NY, 1, LANES), I32),
            pltpu.VMEM((NEAREST, *piece), F32),
            pltpu.VMEM((NEAREST, *piece), F32),
            pltpu.VMEM((nz // NZB, *piece), F32),
            pltpu.VMEM((NEAREST, *piece), F32),
            pltpu.VMEM((ntp // 2, 2, 1, LANES), F32),
            dma((4,)), dma((NY,)), dma((NY,)), dma((nz,)), dma((nz,)), dma((len(PARTS), 7)), dma((len(PARTS), 7)),
            dma((NEAREST,)), dma((NEAREST,)), dma((nz // NZB,)), dma((nz // NZB,)), dma((NEAREST,)), dma((NEAREST,)),
            dma((ntp,)), dma((ntp,)),
        ],
        compiler_params=pltpu.CompilerParams(collective_id=0, has_side_effects=True, vmem_limit_bytes=60 << 20),
        name="mix",
    )(fill, docs, q, k, v, g, ft, taps, skip)


def place_kernel(*refs):
    big, pk_ref, outs, small = refs[:4], refs[4], refs[5:9], refs[9:12]
    held, pk, mix, skip, feat, load, store = refs[12:]
    half = held.shape[1] // 2
    moves = [(i, j, pl.ds(half * j, half)) for j in range(2) for i in range(4)]
    first = pltpu.make_async_copy(pk_ref, pk, load.at[4, 0])
    first.start()
    loads = [pltpu.make_async_copy(big[i].at[part], held.at[i, part], load.at[i, j]) for i, j, part in moves]
    stores = [pltpu.make_async_copy(held.at[i, part], outs[i].at[part], store.at[i, j]) for i, j, part in moves]
    for c in loads:
        c.start()
    first.wait()
    for k in range(pk.shape[0] // 2):
        lanes = slice(LANES * k, LANES * k + LANES)
        mix[8 * k:8 * k + 8, :] = pk[2 * k, 0:8]
        skip[:, lanes] = pk[2 * k, 8:9]
        for w in range(3):
            for j in range(SHORT):
                r = 9 + SHORT * w + j
                feat[w, j:j + 1, lanes] = pk[2 * k + r // 16, r % 16:r % 16 + 1]
    for i, source in enumerate((mix, skip, feat)):
        c = pltpu.make_async_copy(source, small[i], store.at[4 + i, 0])
        c.start()
        stores.append(c)
    for c, d in zip(loads, stores):
        c.wait()
        d.start()
    for d in stores:
        d.wait()


def place_call(big, pk, groups):
    rows, ch = big[0].shape
    hbm = pl.BlockSpec(memory_space=pl.ANY)
    small = ((groups, FILT), (1, ch), (3, SHORT, ch))
    return pl.pallas_call(
        place_kernel,
        out_shape=tuple(jax.ShapeDtypeStruct((rows, ch), BF16) for _ in range(4))
        + tuple(jax.ShapeDtypeStruct(shape, F32) for shape in small),
        in_specs=[hbm] * 5,
        out_specs=(hbm,) * 7,
        scratch_shapes=[pltpu.VMEM((4, rows, ch), BF16), pltpu.VMEM(pk.shape, F32)]
        + [pltpu.VMEM(shape, F32) for shape in small]
        + [pltpu.SemaphoreType.DMA((5, 2)), pltpu.SemaphoreType.DMA((7, 2))],
        compiler_params=pltpu.CompilerParams(vmem_limit_bytes=60 << 20),
        name="place",
    )(*big, pk)


def solution(mesh):
    n, ntp = mesh.shape["ctx"], mesh.shape["tp"]
    nz = n // NY

    def shards(q, k, v, g, fill, docs, ft, taps, skip):
        groups, ch = taps.shape[0], q.shape[1]
        params = (groups * FILT + ch * (1 + 3 * SHORT)) * ntp
        *big, pk = mix_call(nz, ntp, params, fill, docs, q, k, v, g, ft, taps, skip.reshape(1, ch))
        *big, mix_grad, skip_grad, feat_grad = place_call(big, pk, groups)
        return *big, mix_grad, skip_grad.reshape(ch), feat_grad

    rows, whole = P("ctx", "tp"), P(None, None, "tp")
    return jax.shard_map(
        shards, mesh=mesh,
        in_specs=(rows, rows, rows, rows, P("ctx"), P(), whole, P("tp", None), P("tp")),
        out_specs=(rows, rows, rows, rows, P("tp", None), P("tp"), whole),
        check_vma=False)
```

```python
import jax
import jax.numpy as jnp
from jax import lax
from jax.experimental import pallas as pl
from jax.experimental.pallas import tpu as pltpu
from jax.sharding import PartitionSpec as P

F32 = jnp.float32
BF16 = jnp.bfloat16
I32 = jnp.int32
MESH = pl.DeviceIdType.MESH

NY = 4
HALO = 144
NEAR = 16
LANES = 128
SHORT = 7
FILT = 128
GROUP = 16
BIG = 1 << 28

OFF = HALO
QOFF = NEAR
OUT = 272
WIN = 400
MSLOT = 128

NEAREST = 16
NZB = 4
PARTS = ((0, 1), (1, 3), (3, 8))
TAILS = (HALO, HALO, NEAR)


def mesh_copy(src, dst, ssem, rsem, device):
    c = pltpu.make_async_remote_copy(src_ref=src, dst_ref=dst, send_sem=ssem, recv_sem=rsem,
                                     device_id=device, device_id_type=MESH)
    c.start()
    return c


def piece_copy(raw, got, s1, r1, piece, e, device):
    return pltpu.make_async_remote_copy(src_ref=raw.at[piece], dst_ref=got.at[e], send_sem=s1.at[e], recv_sem=r1.at[e],
                                        device_id=device, device_id_type=MESH)


class Peers:
    def __init__(self, nz, ntp):
        self.nz, self.ntp = nz, ntp
        self.me = lax.axis_index("ctx")
        self.tp = lax.axis_index("tp")
        self.z, self.y = self.me // NY, self.me % NY
        self.za, self.zb = self.z // NZB, self.z % NZB
        self.nza = nz // NZB

    def along_y(self, d):
        return {"ctx": self.z * NY + lax.rem(self.y + d, NY)}

    def along_z(self, d):
        return {"ctx": lax.rem(self.z + d, self.nz) * NY + self.y}

    def step(self, d):
        return {"ctx": lax.rem(self.me + d + self.nz * NY, self.nz * NY)}

    def near(self, e):
        y, zb = lax.rem(self.y + e // NZB, NY), lax.rem(self.zb + e % NZB, NZB)
        return y * NZB + zb, {"ctx": (self.za * NZB + zb) * NY + y}

    def far(self, d):
        return {"ctx": (lax.rem(self.za + d, self.nza) * NZB + self.zb) * NY + self.y}

    def owner(self, piece):
        y, zb = piece // NZB, piece % NZB
        e = lax.rem(y - self.y + NY, NY) * NZB + lax.rem(zb - self.zb + NZB, NZB)
        return e, {"ctx": (self.za * NZB + zb) * NY + y}

    def other_core(self):
        return {"tp": self.tp + 1 - 2 * (self.tp % 2)}

    def along_x(self, d):
        return {"tp": lax.rem(self.tp + 2 * d, self.ntp)}


def exchange(at, fill, meanwhile, q_ref, k_ref, v_ref, g_ref, first, hn, hp, vbuf, tails, counts,
             load_sem, ysend, yrecv, zsend, zrecv, hsend, hrecv):
    nz, rows = at.nz, q_ref.shape[0]
    loads = []
    for i, ref in enumerate((q_ref, k_ref, v_ref, g_ref)):
        c = pltpu.make_async_copy(ref, vbuf.at[i], load_sem.at[i])
        c.start()
        loads.append(c)

    barrier = pltpu.get_barrier_semaphore()
    partners = [at.along_y(d) for d in range(1, NY)] + [at.along_z(d) for d in range(1, nz)] + [at.step(1), at.step(-1)]
    partners += [at.near(e)[1] for e in range(1, NEAREST) if e // NZB and e % NZB] + [at.other_core()] + [at.along_x(d) for d in range(1, at.ntp // 2)]
    for device in partners:
        pl.semaphore_signal(barrier, inc=1, device_id=device, device_id_type=MESH)
    counts[at.z, at.y] = jnp.full((1, LANES), fill, I32)
    pl.semaphore_wait(barrier, len(partners))

    own = counts.at[at.z, at.y]
    ycopies = [mesh_copy(own, own, ysend.at[d], yrecv.at[d], at.along_y(d)) for d in range(1, NY)]
    for c in head_copies(at, 0, q_ref, k_ref, v_ref, g_ref, hp, hsend, hrecv):
        c.start()
    row = 0
    for i, count in zip((1, 2, 0), TAILS):
        loads[i].wait()
        slot = lax.broadcasted_iota(I32, (count, rows), 0) + (fill - count)
        pick = (slot == lax.broadcasted_iota(I32, (count, rows), 1)).astype(F32).astype(BF16)
        tails[row:row + count, :] = jnp.dot(pick, vbuf[i], preferred_element_type=F32).astype(BF16)
        row += count
    for c in tail_copies(at, 0, tails, hn, hsend, hrecv):
        c.start()
    for c in ycopies:
        c.wait()
    own = counts.at[at.z]
    zcopies = [mesh_copy(own, own, zsend.at[d], zrecv.at[d], at.along_z(d)) for d in range(1, nz)]
    for part in range(1, len(PARTS)):
        for c in head_copies(at, part, q_ref, k_ref, v_ref, g_ref, hp, hsend, hrecv):
            c.start()
        for c in tail_copies(at, part, tails, hn, hsend, hrecv):
            c.start()
    meanwhile()
    for c in zcopies:
        c.wait()
    loads[3].wait()
    shard = lax.broadcasted_iota(I32, counts.shape, 0) * NY + lax.broadcasted_iota(I32, counts.shape, 1)
    first[...] = jnp.sum(jnp.where(shard < at.me, counts[...], 0), axis=(0, 1))


def head_copies(at, part, q_ref, k_ref, v_ref, g_ref, hp, hsend, hrecv):
    copies, row = [], 0
    cols = pl.ds(PARTS[part][0] * LANES, (PARTS[part][1] - PARTS[part][0]) * LANES)
    for i, (ref, count) in enumerate(((q_ref, HALO), (g_ref, HALO), (k_ref, NEAR), (v_ref, NEAR))):
        copies.append(pltpu.make_async_remote_copy(
            src_ref=ref.at[pl.ds(0, count), cols], dst_ref=hp.at[pl.ds(row, count), cols],
            send_sem=hsend.at[part, i], recv_sem=hrecv.at[part, i], device_id=at.step(-1), device_id_type=MESH))
        row += count
    return copies


def tail_copies(at, part, tails, hn, hsend, hrecv):
    copies, row = [], 0
    cols = pl.ds(PARTS[part][0] * LANES, (PARTS[part][1] - PARTS[part][0]) * LANES)
    for i, count in enumerate(TAILS):
        rows = pl.ds(row, count)
        copies.append(pltpu.make_async_remote_copy(
            src_ref=tails.at[rows, cols], dst_ref=hn.at[rows, cols],
            send_sem=hsend.at[part, 4 + i], recv_sem=hrecv.at[part, 4 + i], device_id=at.step(1), device_id_type=MESH))
        row += count
    return copies


def sum_shards(at, params, meanwhile, raw, got, parts, full, squares, s1, r1, s2, r2, s3, r3, s4, r4, out_ref):
    mine = at.y * NZB + at.zb
    for e in range(1, NEAREST):
        piece, device = at.near(e)
        piece_copy(raw, got, s1, r1, piece, e, device).wait()
    acc = raw[mine]
    for e in range(1, NEAREST):
        acc = acc + got[e]
    parts[at.za] = acc
    own = parts.at[at.za]
    copies = [mesh_copy(own, own, s2.at[d], r2.at[d], at.far(d)) for d in range(1, at.nza)]
    meanwhile()
    for c in copies:
        c.wait()
    acc = parts[0]
    for d in range(1, at.nza):
        acc = acc + parts[d]
    full[mine] = acc
    own = full.at[mine]
    copies = [mesh_copy(own, own, s3.at[e], r3.at[e], at.near(e)[1]) for e in range(1, NEAREST)]
    for c in copies:
        c.wait()
    square = jnp.zeros(full.shape[1:], F32)
    for i in range(NEAREST):
        square = square + full[i] * full[i]
    square = jnp.sum(jnp.sum(square, axis=0, keepdims=True), axis=1, keepdims=True)
    chip, core = at.tp // 2, at.tp % 2
    squares[chip, core] = jnp.broadcast_to(square, (1, LANES))
    own = squares.at[chip, core]
    mesh_copy(own, own, s4.at[0], r4.at[0], at.other_core()).wait()
    own = squares.at[chip]
    copies = [mesh_copy(own, own, s4.at[d], r4.at[d], at.along_x(d)) for d in range(1, at.ntp // 2)]
    for c in copies:
        c.wait()
    factor = lax.rsqrt(jnp.sum(squares[...], axis=(0, 1)) / params + 1e-06)
    for i in range(NEAREST):
        out_ref[i] = full[i] * factor


def mix_kernel(nz, ntp, params, fill_ref, docs_ref, q_ref, k_ref, v_ref, g_ref, ft_ref, taps_ref, skip_ref,
               ho_ref, qg_ref, kg_ref, vg_ref, pk_ref,
               qx, kx, vx, gw, query, keys, values, qb, kb, vb, m, gx, mown, dist, near, maskf, maskb, maskp, shift, taps, vout, stack, pairs, fold,
               first_row, hn, hp, vbuf, tails, counts, raw, got, parts, full, squares,
               load_sem, ysend, yrecv, zsend, zrecv, hsend, hrecv, s1, r1, s2, r2, s3, r3, s4, r4):
    step = pl.program_id(0)
    rows = q_ref.shape[0]
    fill = fill_ref[0]
    peers = Peers(nz, ntp)
    last = peers.me == nz * NY - 1

    @pl.when(step == 0)
    def _():
        def meanwhile():
            r = lax.broadcasted_iota(I32, shift.shape, 0) + 192
            shift[...] = (r - fill == lax.broadcasted_iota(I32, shift.shape, 1)).astype(F32).astype(BF16)
            m[MSLOT + OUT:, :] = jnp.zeros((m.shape[0] - MSLOT - OUT, LANES), BF16)
            gx[WIN:, :] = jnp.zeros((gx.shape[0] - WIN, LANES), BF16)
            taps[...] = taps_ref[...].astype(F32)

        exchange(peers, fill, meanwhile, q_ref, k_ref, v_ref, g_ref, first_row, hn, hp, vbuf, tails, counts,
                 load_sem, ysend, yrecv, zsend, zrecv, hsend, hrecv)
        begin_rows = [docs_ref[i] - first_row[...] for i in range(docs_ref.shape[0])]
        end = jnp.where(last, fill, BIG)

        def doc_begin(slot):
            found = jnp.full(slot.shape, -BIG, I32)
            for b in begin_rows:
                b = jnp.broadcast_to(b[:, 0:1], slot.shape)
                found = jnp.where(slot >= b, jnp.maximum(found, b), found)
            return found

        slot = lax.broadcasted_iota(I32, dist.shape, 0) - MSLOT
        dist[...] = slot - doc_begin(slot)
        slot = lax.broadcasted_iota(I32, near.shape, 0)
        until = jnp.full(slot.shape, BIG, I32)
        for b in begin_rows:
            b = jnp.broadcast_to(b[:, 0:1], slot.shape)
            until = jnp.where(slot < b, jnp.minimum(until, b), until)
        near[...] = jnp.where(slot < fill, jnp.minimum(until, end) - 1 - slot, -1)
        for b, count in ((0, 128), (1, 128), (2, 16)):
            shape = (count, 256)
            a = lax.broadcasted_iota(I32, shape, 0)
            lane = lax.broadcasted_iota(I32, shape, 1)
            far = dist[MSLOT + 128 * b:MSLOT + 128 * b + count, :]
            far = jnp.concatenate([far, far], axis=1)
            j = a + 128 - lane
            keep = (j >= 0) & (j < FILT) & (j <= far)
            maskf[128 * b:128 * b + count, :] = keep.astype(F32).astype(BF16)
            later = 128 * b + lax.broadcasted_iota(I32, (8, 256), 1)
            begin = jnp.where(later < end, doc_begin(later), BIG)
            begin = jnp.broadcast_to(begin[0:1], shape) - 128 * b
            j = lane - a
            keep = (j >= 0) & (j < FILT) & (a >= begin)
            maskb[128 * b:128 * b + count, :] = keep.astype(F32).astype(BF16)
            if b < 2:
                j = lane - 127 + a
                maskp[128 * b:128 * b + count, :] = ((j >= 0) & (j < FILT) & (127 - a >= begin)).astype(F32)

    for part, (begin, _) in enumerate(PARTS):

        @pl.when(step == begin)
        def _():
            for c in head_copies(peers, part, q_ref, k_ref, v_ref, g_ref, hp, hsend, hrecv):
                c.wait()
            for c in tail_copies(peers, part, tails, hn, hsend, hrecv):
                c.wait()

    def own_or_next(i, moved, begin, count):
        slot = lax.broadcasted_iota(I32, (count, LANES), 0) + begin
        return jnp.where(slot < fill, vbuf[i, begin:begin + count, lanes].astype(F32), moved)

    lanes = pl.ds(pl.multiple_of(step * LANES, LANES), LANES)
    kx[0:OFF, :] = hn[0:HALO, lanes].astype(F32)
    vx[0:OFF, :] = hn[HALO:2 * HALO, lanes].astype(F32)
    qx[0:QOFF, :] = hn[2 * HALO:2 * HALO + NEAR, lanes].astype(F32)
    moved_q = jnp.dot(shift[...], hp[0:HALO, lanes], preferred_element_type=F32)
    moved_g = jnp.dot(shift[...], hp[HALO:2 * HALO, lanes], preferred_element_type=F32)
    moved_k = jnp.dot(shift[0:80, 0:NEAR], hp[2 * HALO:2 * HALO + NEAR, lanes], preferred_element_type=F32)
    moved_v = jnp.dot(shift[0:80, 0:NEAR], hp[2 * HALO + NEAR:2 * HALO + 2 * NEAR, lanes], preferred_element_type=F32)
    windows = ((qx, QOFF, moved_q), (kx, OFF, moved_k), (vx, OFF, moved_v), (gw, 0, moved_g))
    for i, (out, off, moved) in enumerate(windows):
        out[off:off + 192, :] = vbuf[i, 0:192, lanes].astype(F32)
        out[off + 192:off + 256, :] = own_or_next(i, moved[0:64], 192, 64)
        out[off + 256:off + 192 + moved.shape[0], :] = moved[64:]

    feat = [ft_ref[w, :, lanes].astype(F32) for w in range(3)]
    block = 16

    def featurize(window, at, far, w):
        acc = feat[w][0:1, :] * window[at:at + block, :]
        for j in range(1, SHORT):
            acc = acc + jnp.where(far >= j, feat[w][j:j + 1, :] * window[at - j:at - j + block, :], 0.0)
        return acc

    for s in range(-MSLOT, OUT, block):
        far = dist[s + MSLOT:s + MSLOT + block, :]
        key_rows = featurize(kx, OFF + s, far, 1)
        value_rows = featurize(vx, OFF + s, far, 2)
        m[MSLOT + s:MSLOT + s + block, :] = (key_rows * value_rows).astype(BF16)
        if s >= 0:
            keys[s:s + block, :] = key_rows
            values[s:s + block, :] = value_rows
    for s in range(0, WIN, block):
        far = dist[s + MSLOT:s + MSLOT + block, :]
        query_rows = featurize(qx, QOFF + s, far, 0)
        gx[s:s + block, :] = (query_rows * gw[s:s + block, :]).astype(BF16)
        if s < rows:
            query[s:s + block, :] = query_rows

    flip = (lax.broadcasted_iota(I32, (128, 128), 0) + lax.broadcasted_iota(I32, (128, 128), 1)) == 127
    for at in range(0, rows, 128):
        inside = lax.broadcasted_iota(I32, (128, 128), 1) + at < fill
        pick = jnp.where(flip & inside, 1.0, 0.0).astype(BF16)
        mown[at:at + 128, :] = jnp.dot(pick, m[MSLOT + at:MSLOT + at + 128, :], preferred_element_type=F32).astype(BF16)

    group_of = lax.broadcasted_iota(I32, (128, LANES), 1) // GROUP
    my_taps = taps[pl.ds(pl.multiple_of(step * 8, 8), 8), :]
    reverse = (lax.broadcasted_iota(I32, (FILT, FILT), 0) + lax.broadcasted_iota(I32, (FILT, FILT), 1)) % FILT == 0
    turned = jnp.dot(my_taps.astype(BF16), reverse.astype(F32).astype(BF16), preferred_element_type=F32)

    def circulant(row):
        return pltpu.roll(jnp.broadcast_to(row, (FILT, FILT)), 0, 1, stride=1, stride_axis=0)

    blocks = ((0, 128), (1, 128), (2, 16))
    skip = skip_ref[:, lanes]

    def banded(rows8, mask, window):
        for g in range(8):
            circ = circulant(rows8[g:g + 1, :]).astype(BF16)
            circ = jnp.concatenate([circ, circ], axis=1)
            for b, count in blocks:
                stack[b, g * count:(g + 1) * count, :] = circ[:count] * mask[128 * b:128 * b + count, :]
        acc = []
        for b, count in blocks:
            res = jnp.dot(stack[b, 0:8 * count, :], window[128 * b:128 * b + 256, :], preferred_element_type=F32)
            out = res[0:count]
            for g in range(1, 8):
                out = jnp.where(group_of[:count] == g, res[g * count:(g + 1) * count], out)
            acc.append(out)
        return acc

    acc = banded(turned, maskf, m)
    for b, count in blocks:
        at = 128 * b
        gated = acc[b] + skip * m[MSLOT + at:MSLOT + at + count, :].astype(F32)
        qb[step, at:at + count, :] = (gw[at:at + count, :] * gated).astype(BF16).astype(F32)
        if b < 2:
            inside = lax.broadcasted_iota(I32, (count, LANES), 0) + at < fill
            vout[0, at:at + count, lanes] = jnp.where(inside, query[at:at + count, :] * gated, 0.0).astype(BF16)

    acc = banded(my_taps, maskb, gx)
    mix_rows = []
    for b in range(2):
        for g in range(8):
            mine = jnp.where(group_of == g, mown[128 * b:128 * b + 128, :], jnp.zeros((), BF16))
            pairs[b, 128 * g:128 * g + 128, :] = mine
    for b in range(2):
        prod = lax.dot_general(pairs[b], gx[128 * b:128 * b + 256, :], (((1,), (1,)), ((), ())), preferred_element_type=F32)
        for g in range(8):
            part = prod[128 * g:128 * g + 128] * maskp[128 * b:128 * b + 128, :]
            part = part[:, :128] + part[:, 128:]
            if b == 0:
                fold[g] = part
            else:
                part = pltpu.roll(part + fold[g], 1, 1, stride=1, stride_axis=0)
                mix_rows.append(jnp.sum(part, axis=0, keepdims=True))
    for b, count in blocks:
        at = 128 * b
        back = acc[b] + skip * gx[at:at + count, :].astype(F32)
        kb[step, at:at + count, :] = (back * values[at:at + count, :]).astype(BF16).astype(F32)
        vb[step, at:at + count, :] = (back * keys[at:at + count, :]).astype(BF16).astype(F32)

    slot = lax.broadcasted_iota(I32, (rows, LANES), 0)
    both = m[MSLOT:MSLOT + rows, :].astype(F32) * gx[0:rows, :].astype(F32)
    skip_row = jnp.sum(jnp.where(slot < fill, both, 0.0), axis=0, keepdims=True)
    feat_rows = []
    for w, (back, window, off) in enumerate(((qb, qx, QOFF), (kb, kx, OFF), (vb, vx, OFF))):
        sums = [jnp.zeros((block, LANES), F32) for _ in range(SHORT)]
        for s in range(0, rows, block):
            reach = near[s:s + block, :]
            source = window[off + s:off + s + block, :]
            for j in range(SHORT):
                later = jnp.where(reach >= j, back[step, s + j:s + j + block, :], 0.0)
                sums[j] = sums[j] + source * later
        feat_rows += [jnp.sum(x, axis=0, keepdims=True) for x in sums]
    packed = jnp.concatenate(mix_rows + [skip_row] + feat_rows + [jnp.zeros((2, LANES), F32)], axis=0)
    for i in range(2):
        piece = 2 * step + i
        raw[piece] = packed[16 * i:16 * i + 16]
        e, device = peers.owner(piece)

        @pl.when(e != 0)
        def _():
            piece_copy(raw, got, s1, r1, piece, e, device).start()

    @pl.when(step == pl.num_programs(0) - 1)
    def _():
        outs = [pltpu.make_async_copy(vout.at[i], ref, load_sem.at[i]) for i, ref in enumerate((ho_ref, qg_ref, kg_ref, vg_ref))]

        def meanwhile():
            outs[0].start()
            for w, back in enumerate((qb, kb, vb)):

                def chunk(i, carry):
                    cols = pl.ds(pl.multiple_of(i * LANES, LANES), LANES)
                    weight = ft_ref[w, :, cols].astype(F32)
                    for s in range(0, rows, block):
                        reach = near[s:s + block, :]
                        acc = jnp.zeros((block, LANES), F32)
                        for j in range(SHORT):
                            later = jnp.where(reach >= j, back[i, s + j:s + j + block, :], 0.0)
                            acc = acc + weight[j:j + 1, :] * later
                        vout[1 + w, s:s + block, cols] = acc.astype(BF16)
                    return carry

                lax.fori_loop(0, pl.num_programs(0), chunk, 0)
                outs[1 + w].start()

        sum_shards(peers, params, meanwhile, raw, got, parts, full, squares, s1, r1, s2, r2, s3, r3, s4, r4, pk_ref)
        for c in outs:
            c.wait()


def mix_call(nz, ntp, params, fill, docs, q, k, v, g, ft, taps, skip):
    rows, ch = q.shape
    steps = ch // LANES
    smem = pl.BlockSpec(memory_space=pltpu.SMEM)
    hbm = pl.BlockSpec(memory_space=pl.ANY)
    dma = pltpu.SemaphoreType.DMA
    piece = (16, LANES)
    return pl.pallas_call(
        lambda *refs: mix_kernel(nz, ntp, params, *refs),
        grid=(steps,),
        out_shape=tuple(jax.ShapeDtypeStruct((rows, ch), BF16) for _ in range(4))
        + (jax.ShapeDtypeStruct((NEAREST, *piece), F32),),
        in_specs=[smem, smem, hbm, hbm, hbm, hbm,
                  pl.BlockSpec(ft.shape, lambda i: (0, 0, 0)), pl.BlockSpec(taps.shape, lambda i: (0, 0)),
                  pl.BlockSpec(skip.shape, lambda i: (0, 0))],
        out_specs=(hbm, hbm, hbm, hbm, pl.BlockSpec((NEAREST, *piece), lambda i: (0, 0, 0))),
        scratch_shapes=[
            pltpu.VMEM((QOFF + WIN, LANES), F32),
            pltpu.VMEM((OFF + OUT, LANES), F32),
            pltpu.VMEM((OFF + OUT, LANES), F32),
            pltpu.VMEM((WIN, LANES), F32),
            pltpu.VMEM((rows, LANES), F32),
            pltpu.VMEM((OUT, LANES), F32),
            pltpu.VMEM((OUT, LANES), F32),
            pltpu.VMEM((steps, OUT, LANES), F32),
            pltpu.VMEM((steps, OUT, LANES), F32),
            pltpu.VMEM((steps, OUT, LANES), F32),
            pltpu.VMEM((512, LANES), BF16),
            pltpu.VMEM((512, LANES), BF16),
            pltpu.VMEM((rows, LANES), BF16),
            pltpu.VMEM((MSLOT + WIN, LANES), I32),
            pltpu.VMEM((rows, LANES), I32),
            pltpu.VMEM((OUT, 256), BF16),
            pltpu.VMEM((OUT, 256), BF16),
            pltpu.VMEM((rows, 256), F32),
            pltpu.VMEM((WIN - 192, HALO), BF16),
            pltpu.VMEM(taps.shape, F32),
            pltpu.VMEM((4, rows, ch), BF16),
            pltpu.VMEM((3, 1024, 256), BF16),
            pltpu.VMEM((2, 1024, LANES), BF16),
            pltpu.VMEM((8, 128, LANES), F32),
            pltpu.VMEM((1, LANES), I32),
            pltpu.VMEM((2 * HALO + NEAR, ch), BF16),
            pltpu.VMEM((2 * HALO + 2 * NEAR, ch), BF16),
            pltpu.VMEM((4, rows, ch), BF16),
            pltpu.VMEM((2 * HALO + NEAR, ch), BF16),
            pltpu.VMEM((nz, NY, 1, LANES), I32),
            pltpu.VMEM((NEAREST, *piece), F32),
            pltpu.VMEM((NEAREST, *piece), F32),
            pltpu.VMEM((nz // NZB, *piece), F32),
            pltpu.VMEM((NEAREST, *piece), F32),
            pltpu.VMEM((ntp // 2, 2, 1, LANES), F32),
            dma((4,)), dma((NY,)), dma((NY,)), dma((nz,)), dma((nz,)), dma((len(PARTS), 7)), dma((len(PARTS), 7)),
            dma((NEAREST,)), dma((NEAREST,)), dma((nz // NZB,)), dma((nz // NZB,)), dma((NEAREST,)), dma((NEAREST,)),
            dma((ntp,)), dma((ntp,)),
        ],
        compiler_params=pltpu.CompilerParams(collective_id=0, has_side_effects=True, vmem_limit_bytes=60 << 20),
        name="mix",
    )(fill, docs, q, k, v, g, ft, taps, skip)


def place_kernel(*refs):
    big, pk_ref, outs, small = refs[:4], refs[4], refs[5:9], refs[9:12]
    held, pk, mix, skip, feat, load, store = refs[12:]
    half = held.shape[1] // 2
    moves = [(i, j, pl.ds(half * j, half)) for j in range(2) for i in range(4)]
    first = pltpu.make_async_copy(pk_ref, pk, load.at[4, 0])
    first.start()
    loads = [pltpu.make_async_copy(big[i].at[part], held.at[i, part], load.at[i, j]) for i, j, part in moves]
    stores = [pltpu.make_async_copy(held.at[i, part], outs[i].at[part], store.at[i, j]) for i, j, part in moves]
    for c in loads:
        c.start()
    first.wait()
    for k in range(pk.shape[0] // 2):
        lanes = slice(LANES * k, LANES * k + LANES)
        mix[8 * k:8 * k + 8, :] = pk[2 * k, 0:8]
        skip[:, lanes] = pk[2 * k, 8:9]
        for w in range(3):
            for j in range(SHORT):
                r = 9 + SHORT * w + j
                feat[w, j:j + 1, lanes] = pk[2 * k + r // 16, r % 16:r % 16 + 1]
    for i, source in enumerate((mix, skip, feat)):
        c = pltpu.make_async_copy(source, small[i], store.at[4 + i, 0])
        c.start()
        stores.append(c)
    for c, d in zip(loads, stores):
        c.wait()
        d.start()
    for d in stores:
        d.wait()


def place_call(big, pk, groups):
    rows, ch = big[0].shape
    hbm = pl.BlockSpec(memory_space=pl.ANY)
    small = ((groups, FILT), (1, ch), (3, SHORT, ch))
    return pl.pallas_call(
        place_kernel,
        out_shape=tuple(jax.ShapeDtypeStruct((rows, ch), BF16) for _ in range(4))
        + tuple(jax.ShapeDtypeStruct(shape, F32) for shape in small),
        in_specs=[hbm] * 5,
        out_specs=(hbm,) * 7,
        scratch_shapes=[pltpu.VMEM((4, rows, ch), BF16), pltpu.VMEM(pk.shape, F32)]
        + [pltpu.VMEM(shape, F32) for shape in small]
        + [pltpu.SemaphoreType.DMA((5, 2)), pltpu.SemaphoreType.DMA((7, 2))],
        compiler_params=pltpu.CompilerParams(vmem_limit_bytes=60 << 20),
        name="place",
    )(*big, pk)


def solution(mesh):
    n, ntp = mesh.shape["ctx"], mesh.shape["tp"]
    nz = n // NY

    def shards(q, k, v, g, fill, docs, ft, taps, skip):
        groups, ch = taps.shape[0], q.shape[1]
        params = (groups * FILT + ch * (1 + 3 * SHORT)) * ntp
        *big, pk = mix_call(nz, ntp, params, fill, docs, q, k, v, g, ft, taps, skip.reshape(1, ch))
        *big, mix_grad, skip_grad, feat_grad = place_call(big, pk, groups)
        return *big, mix_grad, skip_grad.reshape(ch), feat_grad

    rows, whole = P("ctx", "tp"), P(None, None, "tp")
    return jax.shard_map(
        shards, mesh=mesh,
        in_specs=(rows, rows, rows, rows, P("ctx"), P(), whole, P("tp", None), P("tp")),
        out_specs=(rows, rows, rows, rows, P("tp", None), P("tp"), whole),
        check_vma=False)
```

```python
import jax
import jax.numpy as jnp
from jax import lax
from jax.experimental import pallas as pl
from jax.experimental.pallas import tpu as pltpu
from jax.sharding import PartitionSpec as P

F32 = jnp.float32
BF16 = jnp.bfloat16
I32 = jnp.int32
MESH = pl.DeviceIdType.MESH

NY = 4
HALO = 144
NEAR = 16
LANES = 128
SHORT = 7
FILT = 128
GROUP = 16
BIG = 1 << 28

OFF = HALO
QOFF = NEAR
OUT = 272
WIN = 400
MSLOT = 128

NEAREST = 16
NZB = 4
PARTS = ((0, 1), (1, 3), (3, 8))
TAILS = (HALO, HALO, NEAR)


def mesh_copy(src, dst, ssem, rsem, device):
    c = pltpu.make_async_remote_copy(src_ref=src, dst_ref=dst, send_sem=ssem, recv_sem=rsem,
                                     device_id=device, device_id_type=MESH)
    c.start()
    return c


def piece_copy(raw, got, s1, r1, piece, e, device):
    return pltpu.make_async_remote_copy(src_ref=raw.at[piece], dst_ref=got.at[e], send_sem=s1.at[e], recv_sem=r1.at[e],
                                        device_id=device, device_id_type=MESH)


class Peers:
    def __init__(self, nz, ntp):
        self.nz, self.ntp = nz, ntp
        self.me = lax.axis_index("ctx")
        self.tp = lax.axis_index("tp")
        self.z, self.y = self.me // NY, self.me % NY
        self.za, self.zb = self.z // NZB, self.z % NZB
        self.nza = nz // NZB

    def along_y(self, d):
        return {"ctx": self.z * NY + lax.rem(self.y + d, NY)}

    def along_z(self, d):
        return {"ctx": lax.rem(self.z + d, self.nz) * NY + self.y}

    def step(self, d):
        return {"ctx": lax.rem(self.me + d + self.nz * NY, self.nz * NY)}

    def near(self, e):
        y, zb = lax.rem(self.y + e // NZB, NY), lax.rem(self.zb + e % NZB, NZB)
        return y * NZB + zb, {"ctx": (self.za * NZB + zb) * NY + y}

    def far(self, d):
        return {"ctx": (lax.rem(self.za + d, self.nza) * NZB + self.zb) * NY + self.y}

    def owner(self, piece):
        y, zb = piece // NZB, piece % NZB
        e = lax.rem(y - self.y + NY, NY) * NZB + lax.rem(zb - self.zb + NZB, NZB)
        return e, {"ctx": (self.za * NZB + zb) * NY + y}

    def other_core(self):
        return {"tp": self.tp + 1 - 2 * (self.tp % 2)}

    def along_x(self, d):
        return {"tp": lax.rem(self.tp + 2 * d, self.ntp)}


def exchange(at, fill, meanwhile, q_ref, k_ref, v_ref, g_ref, first, hn, hp, vbuf, tails, counts,
             load_sem, ysend, yrecv, zsend, zrecv, hsend, hrecv):
    nz, rows = at.nz, q_ref.shape[0]
    loads = []
    for i, ref in enumerate((q_ref, k_ref, v_ref, g_ref)):
        c = pltpu.make_async_copy(ref, vbuf.at[i], load_sem.at[i])
        c.start()
        loads.append(c)

    barrier = pltpu.get_barrier_semaphore()
    partners = [at.along_y(d) for d in range(1, NY)] + [at.along_z(d) for d in range(1, nz)] + [at.step(1), at.step(-1)]
    partners += [at.near(e)[1] for e in range(1, NEAREST) if e // NZB and e % NZB] + [at.other_core()] + [at.along_x(d) for d in range(1, at.ntp // 2)]
    for device in partners:
        pl.semaphore_signal(barrier, inc=1, device_id=device, device_id_type=MESH)
    counts[at.z, at.y] = jnp.full((1, LANES), fill, I32)
    pl.semaphore_wait(barrier, len(partners))

    own = counts.at[at.z, at.y]
    ycopies = [mesh_copy(own, own, ysend.at[d], yrecv.at[d], at.along_y(d)) for d in range(1, NY)]
    for c in head_copies(at, 0, q_ref, k_ref, v_ref, g_ref, hp, hsend, hrecv):
        c.start()
    row = 0
    for i, count in zip((1, 2, 0), TAILS):
        loads[i].wait()
        slot = lax.broadcasted_iota(I32, (count, rows), 0) + (fill - count)
        pick = (slot == lax.broadcasted_iota(I32, (count, rows), 1)).astype(F32).astype(BF16)
        tails[row:row + count, :] = jnp.dot(pick, vbuf[i], preferred_element_type=F32).astype(BF16)
        row += count
    for c in tail_copies(at, 0, tails, hn, hsend, hrecv):
        c.start()
    for c in ycopies:
        c.wait()
    own = counts.at[at.z]
    zcopies = [mesh_copy(own, own, zsend.at[d], zrecv.at[d], at.along_z(d)) for d in range(1, nz)]
    for part in range(1, len(PARTS)):
        for c in head_copies(at, part, q_ref, k_ref, v_ref, g_ref, hp, hsend, hrecv):
            c.start()
        for c in tail_copies(at, part, tails, hn, hsend, hrecv):
            c.start()
    meanwhile()
    for c in zcopies:
        c.wait()
    loads[3].wait()
    shard = lax.broadcasted_iota(I32, counts.shape, 0) * NY + lax.broadcasted_iota(I32, counts.shape, 1)
    first[...] = jnp.sum(jnp.where(shard < at.me, counts[...], 0), axis=(0, 1))


def head_copies(at, part, q_ref, k_ref, v_ref, g_ref, hp, hsend, hrecv):
    copies, row = [], 0
    cols = pl.ds(PARTS[part][0] * LANES, (PARTS[part][1] - PARTS[part][0]) * LANES)
    for i, (ref, count) in enumerate(((q_ref, HALO), (g_ref, HALO), (k_ref, NEAR), (v_ref, NEAR))):
        copies.append(pltpu.make_async_remote_copy(
            src_ref=ref.at[pl.ds(0, count), cols], dst_ref=hp.at[pl.ds(row, count), cols],
            send_sem=hsend.at[part, i], recv_sem=hrecv.at[part, i], device_id=at.step(-1), device_id_type=MESH))
        row += count
    return copies


def tail_copies(at, part, tails, hn, hsend, hrecv):
    copies, row = [], 0
    cols = pl.ds(PARTS[part][0] * LANES, (PARTS[part][1] - PARTS[part][0]) * LANES)
    for i, count in enumerate(TAILS):
        rows = pl.ds(row, count)
        copies.append(pltpu.make_async_remote_copy(
            src_ref=tails.at[rows, cols], dst_ref=hn.at[rows, cols],
            send_sem=hsend.at[part, 4 + i], recv_sem=hrecv.at[part, 4 + i], device_id=at.step(1), device_id_type=MESH))
        row += count
    return copies


def sum_shards(at, params, meanwhile, raw, got, parts, full, squares, s1, r1, s2, r2, s3, r3, s4, r4, out_ref):
    mine = at.y * NZB + at.zb
    for e in range(1, NEAREST):
        piece, device = at.near(e)
        piece_copy(raw, got, s1, r1, piece, e, device).wait()
    acc = raw[mine]
    for e in range(1, NEAREST):
        acc = acc + got[e]
    parts[at.za] = acc
    own = parts.at[at.za]
    copies = [mesh_copy(own, own, s2.at[d], r2.at[d], at.far(d)) for d in range(1, at.nza)]
    meanwhile()
    for c in copies:
        c.wait()
    acc = parts[0]
    for d in range(1, at.nza):
        acc = acc + parts[d]
    full[mine] = acc
    own = full.at[mine]
    copies = [mesh_copy(own, own, s3.at[e], r3.at[e], at.near(e)[1]) for e in range(1, NEAREST)]
    for c in copies:
        c.wait()
    square = jnp.zeros(full.shape[1:], F32)
    for i in range(NEAREST):
        square = square + full[i] * full[i]
    square = jnp.sum(jnp.sum(square, axis=0, keepdims=True), axis=1, keepdims=True)
    chip, core = at.tp // 2, at.tp % 2
    squares[chip, core] = jnp.broadcast_to(square, (1, LANES))
    own = squares.at[chip, core]
    mesh_copy(own, own, s4.at[0], r4.at[0], at.other_core()).wait()
    own = squares.at[chip]
    copies = [mesh_copy(own, own, s4.at[d], r4.at[d], at.along_x(d)) for d in range(1, at.ntp // 2)]
    for c in copies:
        c.wait()
    factor = lax.rsqrt(jnp.sum(squares[...], axis=(0, 1)) / params + 1e-06)
    for i in range(NEAREST):
        out_ref[i] = full[i] * factor


def mix_kernel(nz, ntp, params, fill_ref, docs_ref, q_ref, k_ref, v_ref, g_ref, ft_ref, taps_ref, skip_ref,
               ho_ref, qg_ref, kg_ref, vg_ref, pk_ref,
               qx, kx, vx, gw, query, keys, values, qb, kb, vb, m, gx, mown, dist, near, maskf, maskb, maskp, shift, taps, vout, stack, pairs, fold, circ,
               first_row, hn, hp, vbuf, tails, counts, raw, got, parts, full, squares,
               load_sem, ysend, yrecv, zsend, zrecv, hsend, hrecv, s1, r1, s2, r2, s3, r3, s4, r4):
    step = pl.program_id(0)
    rows = q_ref.shape[0]
    fill = fill_ref[0]
    peers = Peers(nz, ntp)
    last = peers.me == nz * NY - 1

    @pl.when(step == 0)
    def _():
        def meanwhile():
            r = lax.broadcasted_iota(I32, shift.shape, 0) + 192
            shift[...] = (r - fill == lax.broadcasted_iota(I32, shift.shape, 1)).astype(F32).astype(BF16)
            m[MSLOT + OUT:, :] = jnp.zeros((m.shape[0] - MSLOT - OUT, LANES), BF16)
            gx[WIN:, :] = jnp.zeros((gx.shape[0] - WIN, LANES), BF16)
            taps[...] = taps_ref[...].astype(F32)
            total_rows = lax.broadcasted_iota(I32, (FILT, FILT), 0) + lax.broadcasted_iota(I32, (FILT, FILT), 1)
            reverse = (total_rows % FILT == 0).astype(F32).astype(BF16)

            def filters(k, carry):
                own = taps[pl.ds(pl.multiple_of(k * 8, 8), 8), :]
                turned = jnp.dot(own.astype(BF16), reverse, preferred_element_type=F32)
                for way, rows8 in enumerate((turned, own)):
                    for g in range(8):
                        row = jnp.broadcast_to(rows8[g:g + 1, :], (FILT, FILT))
                        circ[way, k, g] = pltpu.roll(row, 0, 1, stride=1, stride_axis=0).astype(BF16)
                return carry

            lax.fori_loop(0, pl.num_programs(0), filters, 0)

        exchange(peers, fill, meanwhile, q_ref, k_ref, v_ref, g_ref, first_row, hn, hp, vbuf, tails, counts,
                 load_sem, ysend, yrecv, zsend, zrecv, hsend, hrecv)
        begin_rows = [docs_ref[i] - first_row[...] for i in range(docs_ref.shape[0])]
        end = jnp.where(last, fill, BIG)

        def doc_begin(slot):
            found = jnp.full(slot.shape, -BIG, I32)
            for b in begin_rows:
                b = jnp.broadcast_to(b[:, 0:1], slot.shape)
                found = jnp.where(slot >= b, jnp.maximum(found, b), found)
            return found

        slot = lax.broadcasted_iota(I32, dist.shape, 0) - MSLOT
        dist[...] = slot - doc_begin(slot)
        slot = lax.broadcasted_iota(I32, near.shape, 0)
        until = jnp.full(slot.shape, BIG, I32)
        for b in begin_rows:
            b = jnp.broadcast_to(b[:, 0:1], slot.shape)
            until = jnp.where(slot < b, jnp.minimum(until, b), until)
        near[...] = jnp.where(slot < fill, jnp.minimum(until, end) - 1 - slot, -1)
        for b, count in ((0, 128), (1, 128), (2, 16)):
            shape = (count, 256)
            a = lax.broadcasted_iota(I32, shape, 0)
            lane = lax.broadcasted_iota(I32, shape, 1)
            far = dist[MSLOT + 128 * b:MSLOT + 128 * b + count, :]
            far = jnp.concatenate([far, far], axis=1)
            j = a + 128 - lane
            keep = (j >= 0) & (j < FILT) & (j <= far)
            maskf[128 * b:128 * b + count, :] = keep.astype(F32).astype(BF16)
            later = 128 * b + lax.broadcasted_iota(I32, (8, 256), 1)
            begin = jnp.where(later < end, doc_begin(later), BIG)
            begin = jnp.broadcast_to(begin[0:1], shape) - 128 * b
            j = lane - a
            keep = (j >= 0) & (j < FILT) & (a >= begin)
            maskb[128 * b:128 * b + count, :] = keep.astype(F32).astype(BF16)
            if b < 2:
                j = lane - 127 + a
                maskp[128 * b:128 * b + count, :] = ((j >= 0) & (j < FILT) & (127 - a >= begin)).astype(F32)

    for part, (begin, _) in enumerate(PARTS):

        @pl.when(step == begin)
        def _():
            for c in head_copies(peers, part, q_ref, k_ref, v_ref, g_ref, hp, hsend, hrecv):
                c.wait()
            for c in tail_copies(peers, part, tails, hn, hsend, hrecv):
                c.wait()

    def own_or_next(i, moved, begin, count):
        slot = lax.broadcasted_iota(I32, (count, LANES), 0) + begin
        return jnp.where(slot < fill, vbuf[i, begin:begin + count, lanes].astype(F32), moved)

    lanes = pl.ds(pl.multiple_of(step * LANES, LANES), LANES)
    kx[0:OFF, :] = hn[0:HALO, lanes].astype(F32)
    vx[0:OFF, :] = hn[HALO:2 * HALO, lanes].astype(F32)
    qx[0:QOFF, :] = hn[2 * HALO:2 * HALO + NEAR, lanes].astype(F32)
    moved_q = jnp.dot(shift[...], hp[0:HALO, lanes], preferred_element_type=F32)
    moved_g = jnp.dot(shift[...], hp[HALO:2 * HALO, lanes], preferred_element_type=F32)
    moved_k = jnp.dot(shift[0:80, 0:NEAR], hp[2 * HALO:2 * HALO + NEAR, lanes], preferred_element_type=F32)
    moved_v = jnp.dot(shift[0:80, 0:NEAR], hp[2 * HALO + NEAR:2 * HALO + 2 * NEAR, lanes], preferred_element_type=F32)
    windows = ((qx, QOFF, moved_q), (kx, OFF, moved_k), (vx, OFF, moved_v), (gw, 0, moved_g))
    for i, (out, off, moved) in enumerate(windows):
        out[off:off + 192, :] = vbuf[i, 0:192, lanes].astype(F32)
        out[off + 192:off + 256, :] = own_or_next(i, moved[0:64], 192, 64)
        out[off + 256:off + 192 + moved.shape[0], :] = moved[64:]

    feat = [ft_ref[w, :, lanes].astype(F32) for w in range(3)]
    block = 16

    def featurize(window, at, far, w):
        acc = feat[w][0:1, :] * window[at:at + block, :]
        for j in range(1, SHORT):
            acc = acc + jnp.where(far >= j, feat[w][j:j + 1, :] * window[at - j:at - j + block, :], 0.0)
        return acc

    for s in range(-MSLOT, OUT, block):
        far = dist[s + MSLOT:s + MSLOT + block, :]
        key_rows = featurize(kx, OFF + s, far, 1)
        value_rows = featurize(vx, OFF + s, far, 2)
        m[MSLOT + s:MSLOT + s + block, :] = (key_rows * value_rows).astype(BF16)
        if s >= 0:
            keys[s:s + block, :] = key_rows
            values[s:s + block, :] = value_rows
    for s in range(0, WIN, block):
        far = dist[s + MSLOT:s + MSLOT + block, :]
        query_rows = featurize(qx, QOFF + s, far, 0)
        gx[s:s + block, :] = (query_rows * gw[s:s + block, :]).astype(BF16)
        if s < rows:
            query[s:s + block, :] = query_rows

    flip = (lax.broadcasted_iota(I32, (128, 128), 0) + lax.broadcasted_iota(I32, (128, 128), 1)) == 127
    for at in range(0, rows, 128):
        inside = lax.broadcasted_iota(I32, (128, 128), 1) + at < fill
        pick = jnp.where(flip & inside, 1.0, 0.0).astype(BF16)
        mown[at:at + 128, :] = jnp.dot(pick, m[MSLOT + at:MSLOT + at + 128, :], preferred_element_type=F32).astype(BF16)

    group_of = lax.broadcasted_iota(I32, (128, LANES), 1) // GROUP
    blocks = ((0, 128), (1, 128), (2, 16))
    skip = skip_ref[:, lanes]

    def banded(way, mask, window):
        for g in range(8):
            both = jnp.concatenate([circ[way, step, g], circ[way, step, g]], axis=1)
            for b, count in blocks:
                stack[b, g * count:(g + 1) * count, :] = both[:count] * mask[128 * b:128 * b + count, :]
        acc = []
        for b, count in blocks:
            res = jnp.dot(stack[b, 0:8 * count, :], window[128 * b:128 * b + 256, :], preferred_element_type=F32)
            out = res[0:count]
            for g in range(1, 8):
                out = jnp.where(group_of[:count] == g, res[g * count:(g + 1) * count], out)
            acc.append(out)
        return acc

    acc = banded(0, maskf, m)
    for b, count in blocks:
        at = 128 * b
        gated = acc[b] + skip * m[MSLOT + at:MSLOT + at + count, :].astype(F32)
        qb[step, at:at + count, :] = (gw[at:at + count, :] * gated).astype(BF16).astype(F32)
        if b < 2:
            inside = lax.broadcasted_iota(I32, (count, LANES), 0) + at < fill
            vout[0, at:at + count, lanes] = jnp.where(inside, query[at:at + count, :] * gated, 0.0).astype(BF16)

    acc = banded(1, maskb, gx)
    mix_rows = []
    for b in range(2):
        for g in range(8):
            mine = jnp.where(group_of == g, mown[128 * b:128 * b + 128, :], jnp.zeros((), BF16))
            pairs[b, 128 * g:128 * g + 128, :] = mine
    for b in range(2):
        prod = lax.dot_general(pairs[b], gx[128 * b:128 * b + 256, :], (((1,), (1,)), ((), ())), preferred_element_type=F32)
        for g in range(8):
            part = prod[128 * g:128 * g + 128] * maskp[128 * b:128 * b + 128, :]
            part = part[:, :128] + part[:, 128:]
            if b == 0:
                fold[g] = part
            else:
                part = pltpu.roll(part + fold[g], 1, 1, stride=1, stride_axis=0)
                mix_rows.append(jnp.sum(part, axis=0, keepdims=True))
    for b, count in blocks:
        at = 128 * b
        back = acc[b] + skip * gx[at:at + count, :].astype(F32)
        kb[step, at:at + count, :] = (back * values[at:at + count, :]).astype(BF16).astype(F32)
        vb[step, at:at + count, :] = (back * keys[at:at + count, :]).astype(BF16).astype(F32)

    slot = lax.broadcasted_iota(I32, (rows, LANES), 0)
    both = m[MSLOT:MSLOT + rows, :].astype(F32) * gx[0:rows, :].astype(F32)
    skip_row = jnp.sum(jnp.where(slot < fill, both, 0.0), axis=0, keepdims=True)
    feat_rows = []
    for w, (back, window, off) in enumerate(((qb, qx, QOFF), (kb, kx, OFF), (vb, vx, OFF))):
        sums = [jnp.zeros((block, LANES), F32) for _ in range(SHORT)]
        for s in range(0, rows, block):
            reach = near[s:s + block, :]
            source = window[off + s:off + s + block, :]
            for j in range(SHORT):
                later = jnp.where(reach >= j, back[step, s + j:s + j + block, :], 0.0)
                sums[j] = sums[j] + source * later
        feat_rows += [jnp.sum(x, axis=0, keepdims=True) for x in sums]
    packed = jnp.concatenate(mix_rows + [skip_row] + feat_rows + [jnp.zeros((2, LANES), F32)], axis=0)
    for i in range(2):
        piece = 2 * step + i
        raw[piece] = packed[16 * i:16 * i + 16]
        e, device = peers.owner(piece)

        @pl.when(e != 0)
        def _():
            piece_copy(raw, got, s1, r1, piece, e, device).start()

    @pl.when(step == pl.num_programs(0) - 1)
    def _():
        outs = [pltpu.make_async_copy(vout.at[i], ref, load_sem.at[i]) for i, ref in enumerate((ho_ref, qg_ref, kg_ref, vg_ref))]

        def meanwhile():
            outs[0].start()
            for w, back in enumerate((qb, kb, vb)):

                def chunk(i, carry):
                    cols = pl.ds(pl.multiple_of(i * LANES, LANES), LANES)
                    weight = ft_ref[w, :, cols].astype(F32)
                    for s in range(0, rows, block):
                        reach = near[s:s + block, :]
                        acc = jnp.zeros((block, LANES), F32)
                        for j in range(SHORT):
                            later = jnp.where(reach >= j, back[i, s + j:s + j + block, :], 0.0)
                            acc = acc + weight[j:j + 1, :] * later
                        vout[1 + w, s:s + block, cols] = acc.astype(BF16)
                    return carry

                lax.fori_loop(0, pl.num_programs(0), chunk, 0)
                outs[1 + w].start()

        sum_shards(peers, params, meanwhile, raw, got, parts, full, squares, s1, r1, s2, r2, s3, r3, s4, r4, pk_ref)
        for c in outs:
            c.wait()


def mix_call(nz, ntp, params, fill, docs, q, k, v, g, ft, taps, skip):
    rows, ch = q.shape
    steps = ch // LANES
    smem = pl.BlockSpec(memory_space=pltpu.SMEM)
    hbm = pl.BlockSpec(memory_space=pl.ANY)
    dma = pltpu.SemaphoreType.DMA
    piece = (16, LANES)
    return pl.pallas_call(
        lambda *refs: mix_kernel(nz, ntp, params, *refs),
        grid=(steps,),
        out_shape=tuple(jax.ShapeDtypeStruct((rows, ch), BF16) for _ in range(4))
        + (jax.ShapeDtypeStruct((NEAREST, *piece), F32),),
        in_specs=[smem, smem, hbm, hbm, hbm, hbm,
                  pl.BlockSpec(ft.shape, lambda i: (0, 0, 0)), pl.BlockSpec(taps.shape, lambda i: (0, 0)),
                  pl.BlockSpec(skip.shape, lambda i: (0, 0))],
        out_specs=(hbm, hbm, hbm, hbm, pl.BlockSpec((NEAREST, *piece), lambda i: (0, 0, 0))),
        scratch_shapes=[
            pltpu.VMEM((QOFF + WIN, LANES), F32),
            pltpu.VMEM((OFF + OUT, LANES), F32),
            pltpu.VMEM((OFF + OUT, LANES), F32),
            pltpu.VMEM((WIN, LANES), F32),
            pltpu.VMEM((rows, LANES), F32),
            pltpu.VMEM((OUT, LANES), F32),
            pltpu.VMEM((OUT, LANES), F32),
            pltpu.VMEM((steps, OUT, LANES), F32),
            pltpu.VMEM((steps, OUT, LANES), F32),
            pltpu.VMEM((steps, OUT, LANES), F32),
            pltpu.VMEM((512, LANES), BF16),
            pltpu.VMEM((512, LANES), BF16),
            pltpu.VMEM((rows, LANES), BF16),
            pltpu.VMEM((MSLOT + WIN, LANES), I32),
            pltpu.VMEM((rows, LANES), I32),
            pltpu.VMEM((OUT, 256), BF16),
            pltpu.VMEM((OUT, 256), BF16),
            pltpu.VMEM((rows, 256), F32),
            pltpu.VMEM((WIN - 192, HALO), BF16),
            pltpu.VMEM(taps.shape, F32),
            pltpu.VMEM((4, rows, ch), BF16),
            pltpu.VMEM((3, 1024, 256), BF16),
            pltpu.VMEM((2, 1024, LANES), BF16),
            pltpu.VMEM((8, 128, LANES), F32),
            pltpu.VMEM((2, steps, 8, FILT, FILT), BF16),
            pltpu.VMEM((1, LANES), I32),
            pltpu.VMEM((2 * HALO + NEAR, ch), BF16),
            pltpu.VMEM((2 * HALO + 2 * NEAR, ch), BF16),
            pltpu.VMEM((4, rows, ch), BF16),
            pltpu.VMEM((2 * HALO + NEAR, ch), BF16),
            pltpu.VMEM((nz, NY, 1, LANES), I32),
            pltpu.VMEM((NEAREST, *piece), F32),
            pltpu.VMEM((NEAREST, *piece), F32),
            pltpu.VMEM((nz // NZB, *piece), F32),
            pltpu.VMEM((NEAREST, *piece), F32),
            pltpu.VMEM((ntp // 2, 2, 1, LANES), F32),
            dma((4,)), dma((NY,)), dma((NY,)), dma((nz,)), dma((nz,)), dma((len(PARTS), 7)), dma((len(PARTS), 7)),
            dma((NEAREST,)), dma((NEAREST,)), dma((nz // NZB,)), dma((nz // NZB,)), dma((NEAREST,)), dma((NEAREST,)),
            dma((ntp,)), dma((ntp,)),
        ],
        compiler_params=pltpu.CompilerParams(collective_id=0, has_side_effects=True, vmem_limit_bytes=60 << 20),
        name="mix",
    )(fill, docs, q, k, v, g, ft, taps, skip)


def place_kernel(*refs):
    big, pk_ref, outs, small = refs[:4], refs[4], refs[5:9], refs[9:12]
    held, pk, mix, skip, feat, load, store = refs[12:]
    part = held.shape[1] // 4
    moves = [(i, j, pl.ds(part * j, part)) for j in range(4) for i in range(4)]
    first = pltpu.make_async_copy(pk_ref, pk, load.at[4, 0])
    first.start()
    loads = [pltpu.make_async_copy(big[i].at[at], held.at[i, at], load.at[i, j]) for i, j, at in moves]
    stores = [pltpu.make_async_copy(held.at[i, at], outs[i].at[at], store.at[i, j]) for i, j, at in moves]
    for c in loads:
        c.start()
    first.wait()
    for k in range(pk.shape[0] // 2):
        lanes = slice(LANES * k, LANES * k + LANES)
        mix[8 * k:8 * k + 8, :] = pk[2 * k, 0:8]
        skip[:, lanes] = pk[2 * k, 8:9]
        for w in range(3):
            for j in range(SHORT):
                r = 9 + SHORT * w + j
                feat[w, j:j + 1, lanes] = pk[2 * k + r // 16, r % 16:r % 16 + 1]
    for i, source in enumerate((mix, skip, feat)):
        c = pltpu.make_async_copy(source, small[i], store.at[4 + i, 0])
        c.start()
        stores.append(c)
    for c, d in zip(loads, stores):
        c.wait()
        d.start()
    for d in stores:
        d.wait()


def place_call(big, pk, groups):
    rows, ch = big[0].shape
    hbm = pl.BlockSpec(memory_space=pl.ANY)
    small = ((groups, FILT), (1, ch), (3, SHORT, ch))
    return pl.pallas_call(
        place_kernel,
        out_shape=tuple(jax.ShapeDtypeStruct((rows, ch), BF16) for _ in range(4))
        + tuple(jax.ShapeDtypeStruct(shape, F32) for shape in small),
        in_specs=[hbm] * 5,
        out_specs=(hbm,) * 7,
        scratch_shapes=[pltpu.VMEM((4, rows, ch), BF16), pltpu.VMEM(pk.shape, F32)]
        + [pltpu.VMEM(shape, F32) for shape in small]
        + [pltpu.SemaphoreType.DMA((5, 4)), pltpu.SemaphoreType.DMA((7, 4))],
        compiler_params=pltpu.CompilerParams(vmem_limit_bytes=60 << 20),
        name="place",
    )(*big, pk)


def solution(mesh):
    n, ntp = mesh.shape["ctx"], mesh.shape["tp"]
    nz = n // NY

    def shards(q, k, v, g, fill, docs, ft, taps, skip):
        groups, ch = taps.shape[0], q.shape[1]
        params = (groups * FILT + ch * (1 + 3 * SHORT)) * ntp
        *big, pk = mix_call(nz, ntp, params, fill, docs, q, k, v, g, ft, taps, skip.reshape(1, ch))
        *big, mix_grad, skip_grad, feat_grad = place_call(big, pk, groups)
        return *big, mix_grad, skip_grad.reshape(ch), feat_grad

    rows, whole = P("ctx", "tp"), P(None, None, "tp")
    return jax.shard_map(
        shards, mesh=mesh,
        in_specs=(rows, rows, rows, rows, P("ctx"), P(), whole, P("tp", None), P("tp")),
        out_specs=(rows, rows, rows, rows, P("tp", None), P("tp"), whole),
        check_vma=False)
```
